256 devices in a mesh: ctx: 64 (over y, z, core), head: 4 (over x).
Axes of the slice: x: 4, y: 4, z: 8, core: 2. Of those that a mesh axis runs over, the one named last changes fastest.
Arguments:
- queries: bfloat16 [16384, 4096], P('ctx', 'head'), may hold values from -6 to 6
- keys: bfloat16 [16384, 4096], P('ctx', 'head'), may hold values from -6 to 6
- values: bfloat16 [16384, 4096], P('ctx', 'head'), may hold values from -150 to 150
- out_grad: bfloat16 [16384, 4096], P('ctx', 'head'), may hold values from -6 to 6
- gain: bfloat16 [4096], P('head'), may hold values from 0.099609375 to 1.8984375
Outputs:
- query_grad: bfloat16 [16384, 4096], P('ctx', 'head')
- key_grad: bfloat16 [16384, 4096], P('ctx', 'head')
- value_grad: bfloat16 [16384, 4096], P('ctx', 'head')
The draws below stay inside these ranges and needn't reach their ends.
All inputs are finite; a program needn't handle non-finite values.
Results may differ from the reference program's by a relative error of at most 0.0058.
Values sent between devices are 32-bit elements; how exact they have to be, the bound alone decides.
No kernel may reach another device: no remote copies, remote signals or barrier semaphores. Data moves between devices by JAX's collectives and lax.ppermute only.
A program may use at most 128 MiB of HBM per device.

```python
import math
import jax
import jax.numpy as jnp
from jax import lax

HEADS = 32
HEAD_DIM = 128
BLOCK = 128
SEQ = 16384


def draw_values(key, part):
    key = jax.random.fold_in(key, 7)
    head_key, row_key, noise_key = jax.random.split(key, 3)
    head_pos = jnp.arange(HEADS, dtype=jnp.float32) / max(HEADS - 1, 1)
    head_scale = 10.0 ** head_pos * jnp.exp(jax.random.uniform(head_key, (HEADS,), jnp.float32, math.log(0.8), math.log(1.25)))
    row_scale = jnp.exp(jax.random.uniform(row_key, (SEQ,), jnp.float32, 0.0, math.log(3.0)))
    noise = jnp.clip(jax.random.normal(noise_key, (SEQ, HEADS, HEAD_DIM), jnp.float32), -4.0, 4.0)
    scaled = noise * head_scale[None, :, None] * row_scale[:, None, None]
    return scaled.reshape(SEQ, HEADS * HEAD_DIM).astype(jnp.bfloat16)


def level_of(stream_key, dims, cuts, low, top_value):
    loudness, own = 1.0, jax.random.fold_in(stream_key, 6)
    for axis_at, parts in cuts:
        draws = jnp.exp(jax.random.uniform(jax.random.fold_in(own, axis_at), (parts,), jnp.float32, low / len(cuts), top_value / len(cuts)))
        loudness = loudness * jnp.repeat(draws, dims[axis_at] // parts).reshape([-1 if axis == axis_at else 1 for axis in range(len(dims))])
    return loudness


def scatter_about(own_key, dims, scale, reach, pieces=(), kind=jnp.bfloat16):
    values = scale * jax.random.normal(own_key, dims, jnp.float32)
    if pieces:
        values = values * level_of(own_key, dims, pieces, -0.22, 0.18)
    return jnp.clip(values, -reach, reach).astype(kind)


def setup_inputs(seed: int = 0) -> dict:
    key_of = jax.random.split(jax.random.key(seed), 6)
    queries = scatter_about(key_of[0], (SEQ, HEADS * HEAD_DIM), 1.0, 6.0, ((0, 64), (1, 4)))
    keys = scatter_about(key_of[1], (SEQ, HEADS * HEAD_DIM), 1.0, 6.0, ((0, 64), (1, 4)))
    values = draw_values(jax.random.fold_in(key_of[5], 71), 0)
    out_grad = scatter_about(key_of[3], (SEQ, HEADS * HEAD_DIM), 1.0, 6.0, ((0, 64), (1, 4)))
    gain = jnp.clip(1.0 + 0.18 * jax.random.normal(key_of[4], (HEADS * HEAD_DIM,), jnp.float32), 0.099609375, 1.8984375).astype(jnp.bfloat16)
    return {"queries": queries, "keys": keys, "values": values, "out_grad": out_grad, "gain": gain}


EPSILON = 1e-05

def causal_mask(size):
    row_index = lax.broadcasted_iota(jnp.int32, (size, size), 0)
    col_index = lax.broadcasted_iota(jnp.int32, (size, size), 1)
    return col_index <= row_index

def to_low(array):
    rounded = lax.optimization_barrier(array.astype(jnp.bfloat16))
    return rounded.astype(jnp.float32)

def reference(queries, keys, values, out_grad, gain):
    factor = HEAD_DIM ** (-0.5)
    blocks = SEQ // BLOCK
    shape = (blocks, BLOCK, HEADS, HEAD_DIM)
    query_blocks = queries.reshape(shape)
    key_blocks = keys.reshape(shape)
    value_blocks = values.reshape(shape)
    grad_blocks = out_grad.reshape(shape)
    causal = causal_mask(BLOCK)[None]
    gain_wide = gain.astype(jnp.float32).reshape(HEADS, HEAD_DIM)

    def block_scores(query_wide, key_wide):
        raw = jnp.einsum('thd,shd->hts', query_wide, key_wide) * factor
        return to_low(jnp.where(causal, raw, 0.0))

    def delta_scores_of(delta_wide, value_wide):
        raw = jnp.einsum('thj,shj->hts', delta_wide, value_wide) * factor
        return to_low(jnp.where(causal, raw, 0.0))

    def forward_step(state, inputs):
        query_block, key_block, value_block, grad_block = inputs
        query_wide = query_block.astype(jnp.float32)
        key_wide = key_block.astype(jnp.float32)
        value_wide = value_block.astype(jnp.float32)
        probs = block_scores(query_wide, key_wide)
        state_low = to_low(state)
        output = jnp.einsum('hts,shd->thd', probs, value_wide) + factor * jnp.einsum('thi,hij->thj', query_wide, state_low)
        squares = lax.optimization_barrier(jnp.mean(output * output, axis=(1, 2)))
        inv_rms = lax.rsqrt(squares + EPSILON)
        upstream = grad_block.astype(jnp.float32) * gain_wide[None]
        mixed = lax.optimization_barrier(jnp.mean(upstream * output, axis=(1, 2)))
        delta = inv_rms[:, None, None] * upstream - (inv_rms ** 3 * mixed)[:, None, None] * output
        delta_wide = to_low(delta)
        delta_scores = delta_scores_of(delta_wide, value_wide)
        query_grad = jnp.einsum('hts,shi->thi', delta_scores, key_wide) + factor * jnp.einsum('thj,hij->thi', delta_wide, state_low)
        new_state = state + jnp.einsum('shi,shj->hij', key_wide, value_wide)
        return (new_state, (query_grad.astype(jnp.bfloat16), delta_wide.astype(jnp.bfloat16)))
    zero_state = jnp.zeros((HEADS, HEAD_DIM, HEAD_DIM), jnp.float32)
    final_state, outputs = lax.scan(forward_step, zero_state, (query_blocks, key_blocks, value_blocks, grad_blocks))
    query_grad, delta_blocks = outputs

    def backward_step(state, inputs):
        query_block, key_block, value_block, delta_block = inputs
        query_wide = query_block.astype(jnp.float32)
        key_wide = key_block.astype(jnp.float32)
        value_wide = value_block.astype(jnp.float32)
        delta_wide = delta_block.astype(jnp.float32)
        probs = block_scores(query_wide, key_wide)
        delta_scores = delta_scores_of(delta_wide, value_wide)
        state_low = to_low(state)
        key_grad = jnp.einsum('hts,thi->shi', delta_scores, query_wide) + factor * jnp.einsum('shj,hji->shi', value_wide, state_low)
        value_grad = jnp.einsum('hts,thj->shj', probs, delta_wide) + factor * jnp.einsum('shi,hji->shj', key_wide, state_low)
        new_state = state + jnp.einsum('thj,thi->hji', delta_wide, query_wide)
        return (new_state, (key_grad.astype(jnp.bfloat16), value_grad.astype(jnp.bfloat16)))
    first_state, grads = lax.scan(backward_step, zero_state, (query_blocks, key_blocks, value_blocks, delta_blocks), reverse=True)
    key_grad, value_grad = grads
    width = HEADS * HEAD_DIM
    return (query_grad.reshape(SEQ, width), key_grad.reshape(SEQ, width), value_grad.reshape(SEQ, width))
```

```python
import functools

import jax
import jax.numpy as jnp
from jax import lax
from jax.experimental import pallas as pl
from jax.experimental.pallas import tpu as pltpu
from jax.sharding import Mesh
from jax.sharding import PartitionSpec as P

HEADS = 32
HEAD_DIM = 128
EPSILON = 1e-05
FEATURES = HEADS * HEAD_DIM
FACTOR = HEAD_DIM ** (-0.5)
F32 = jnp.float32
BF16 = jnp.bfloat16
VMEM_LIMIT = 48 * 1024 * 1024


def dot_nn(a, b):
    return lax.dot_general(a, b, (((1,), (0,)), ((), ())), preferred_element_type=F32)


def dot_nt(a, b):
    return lax.dot_general(a, b, (((1,), (1,)), ((), ())), preferred_element_type=F32)


def dot_tn(a, b):
    return lax.dot_general(a, b, (((0,), (0,)), ((), ())), preferred_element_type=F32)


def columns(head):
    return pl.ds(head * HEAD_DIM, HEAD_DIM)


def causal(count, transposed):
    row = lax.broadcasted_iota(jnp.int32, (count, count), 0)
    col = lax.broadcasted_iota(jnp.int32, (count, count), 1)
    return row <= col if transposed else col <= row


def scores(a, b, mask):
    return jnp.where(mask, dot_nt(a, b) * FACTOR, 0.0).astype(BF16)


def call(kernel, out_shape, **kwargs):
    return pl.pallas_call(
        kernel,
        out_shape=out_shape,
        compiler_params=pltpu.CompilerParams(vmem_limit_bytes=VMEM_LIMIT),
        **kwargs,
    )


def totals_kernel(keys, values, out):
    for head in range(out.shape[0]):
        out[head] = dot_tn(keys[:, columns(head)], values[:, columns(head)])


def scan_kernel(reverse, parts, out):
    count = parts.shape[0]
    order = range(count - 1, -1, -1) if reverse else range(count)
    total = jnp.zeros(parts.shape[1:], F32)
    for at in order:
        out[at] = total
        total = total + parts[at]


def forward_kernel(queries, keys, values, out_grad, gain, state, output, low, sums):
    tokens = queries.shape[0]
    mask = causal(tokens, False)
    square = jnp.zeros((tokens, HEAD_DIM), F32)
    mixed = jnp.zeros((tokens, HEAD_DIM), F32)
    for head in range(state.shape[0]):
        at = columns(head)
        query = queries[:, at]
        probs = scores(query, keys[:, at], mask)
        state_low = state[head].astype(BF16)
        low[head] = state_low
        out = dot_nn(probs, values[:, at]) + FACTOR * dot_nn(query, state_low)
        output[:, at] = out
        upstream = out_grad[:, at].astype(F32) * gain[:, at].astype(F32)
        square = square + out * out
        mixed = mixed + upstream * out
    sums[0:1] = jnp.sum(square.T, axis=0, keepdims=True)
    sums[1:2] = jnp.sum(mixed.T, axis=0, keepdims=True)


def delta_kernel(queries, keys, values, out_grad, gain, output, low, sums, delta, back, query_grad):
    tokens = queries.shape[0]
    mask = causal(tokens, False)
    inv_rms = lax.rsqrt(sums[0:1] / FEATURES + EPSILON)
    pull = inv_rms * inv_rms * inv_rms * (sums[1:2] / FEATURES)
    inv_rms = jnp.broadcast_to(inv_rms, (HEAD_DIM, tokens)).T
    pull = jnp.broadcast_to(pull, (HEAD_DIM, tokens)).T
    for head in range(low.shape[0]):
        at = columns(head)
        upstream = out_grad[:, at].astype(F32) * gain[:, at].astype(F32)
        out_delta = (inv_rms * upstream - pull * output[:, at]).astype(BF16)
        delta[:, at] = out_delta
        back[head] = dot_tn(out_delta, queries[:, at])
        delta_scores = scores(out_delta, values[:, at], mask)
        grad = dot_nn(delta_scores, keys[:, at]) + FACTOR * dot_nt(out_delta, low[head])
        query_grad[:, at] = grad.astype(BF16)


def backward_kernel(queries, keys, values, delta, state, key_grad, value_grad):
    tokens = queries.shape[0]
    mask = causal(tokens, True)
    for head in range(state.shape[0]):
        at = columns(head)
        query, key, value, out_delta = queries[:, at], keys[:, at], values[:, at], delta[:, at]
        later_low = state[head].astype(BF16)
        delta_scores = scores(value, out_delta, mask)
        grad = dot_nn(delta_scores, query) + FACTOR * dot_nn(value, later_low)
        key_grad[:, at] = grad.astype(BF16)
        probs = scores(key, query, mask)
        grad = dot_nn(probs, out_delta) + FACTOR * dot_nt(key, later_low)
        value_grad[:, at] = grad.astype(BF16)


def entering(total, reverse):
    chips = lax.axis_size("chip")
    core = lax.axis_index("core")
    heads = total.shape[0]
    half = heads // 2
    rows = half * HEAD_DIM // chips
    swap = [(0, 1), (1, 0)]
    mine = lax.dynamic_slice_in_dim(total, core * half, half)
    other = lax.dynamic_slice_in_dim(total, (1 - core) * half, half)
    got = lax.ppermute(other, "core", swap)
    parts = (mine + got).reshape(chips, rows, HEAD_DIM)
    parts = lax.all_to_all(parts, "chip", 0, 0, tiled=True)
    parts = call(
        functools.partial(scan_kernel, reverse), jax.ShapeDtypeStruct(parts.shape, F32)
    )(parts)
    pair = lax.all_to_all(parts, "chip", 0, 0, tiled=True).reshape(half, HEAD_DIM, HEAD_DIM)
    ahead = core == (1 if reverse else 0)
    own = pair + jnp.where(ahead, 0.0, got)
    theirs = lax.ppermute(pair + jnp.where(ahead, mine, 0.0), "core", swap)
    return jnp.where(
        core == 0, jnp.concatenate([own, theirs]), jnp.concatenate([theirs, own])
    )


def on_device(queries, keys, values, out_grad, gain):
    tokens, width = queries.shape
    heads = width // HEAD_DIM
    gain = gain.reshape(1, width)
    wide = jax.ShapeDtypeStruct((tokens, width), BF16)
    states = jax.ShapeDtypeStruct((heads, HEAD_DIM, HEAD_DIM), F32)
    total = call(totals_kernel, states)(keys, values)
    state = entering(total, False)
    output, low, sums = call(
        forward_kernel,
        (
            jax.ShapeDtypeStruct((tokens, width), F32),
            jax.ShapeDtypeStruct(states.shape, BF16),
            jax.ShapeDtypeStruct((2, tokens), F32),
        ),
    )(queries, keys, values, out_grad, gain, state)
    sums = lax.psum(sums, "head")
    delta, back, query_grad = call(delta_kernel, (wide, states, wide))(
        queries, keys, values, out_grad, gain, output, low, sums
    )
    state = entering(back, True)
    key_grad, value_grad = call(backward_kernel, (wide, wide))(
        queries, keys, values, delta, state
    )
    return query_grad, key_grad, value_grad


def solution(mesh):
    count, across = mesh.devices.shape
    inner = Mesh(mesh.devices.reshape(count // 2, 2, across), ("chip", "core", "head"))
    spec = P(("chip", "core"), "head")
    return jax.shard_map(
        on_device,
        mesh=inner,
        in_specs=(spec, spec, spec, spec, P("head")),
        out_specs=(spec, spec, spec),
        check_vma=False,
    )
```

```python
import functools

import jax
import jax.numpy as jnp
from jax import lax
from jax.experimental import pallas as pl
from jax.experimental.pallas import tpu as pltpu
from jax.sharding import Mesh
from jax.sharding import PartitionSpec as P

HEADS = 32
HEAD_DIM = 128
EPSILON = 1e-05
FEATURES = HEADS * HEAD_DIM
FACTOR = HEAD_DIM ** (-0.5)
F32 = jnp.float32
BF16 = jnp.bfloat16
VMEM_LIMIT = 16 * 1024 * 1024


def dot_nn(a, b):
    return lax.dot_general(a, b, (((1,), (0,)), ((), ())), preferred_element_type=F32)


def dot_nt(a, b):
    return lax.dot_general(a, b, (((1,), (1,)), ((), ())), preferred_element_type=F32)


def dot_tn(a, b):
    return lax.dot_general(a, b, (((0,), (0,)), ((), ())), preferred_element_type=F32)


def columns(head):
    return pl.ds(head * HEAD_DIM, HEAD_DIM)


def causal(count, transposed):
    row = lax.broadcasted_iota(jnp.int32, (count, count), 0)
    col = lax.broadcasted_iota(jnp.int32, (count, count), 1)
    return row <= col if transposed else col <= row


def scores(a, b, mask):
    return jnp.where(mask, dot_nt(a, b) * FACTOR, 0.0).astype(BF16)


def here(name):
    return lax.axis_index(name)


def near(shape, dtype=F32):
    return pltpu.VMEM(shape, dtype)


def call(kernel, out_shape, far=0, **kwargs):
    def run(*operands):
        spaces = [pltpu.HBM] * far + [pltpu.VMEM] * (len(operands) - far)
        return pl.pallas_call(
            kernel,
            out_shape=out_shape,
            in_specs=[pl.BlockSpec(memory_space=space) for space in spaces],
            compiler_params=pltpu.CompilerParams(vmem_limit_bytes=VMEM_LIMIT),
            **kwargs,
        )(*map(pltpu.with_memory_space_constraint, operands, spaces))

    return run


def totals_kernel(keys_far, values_far, mine, other, keys, values, sems):
    heads = mine.shape[0]
    half = heads * HEAD_DIM
    copies = []
    for part in range(2):
        core = here("core") if part else 1 - here("core")
        there = pl.ds(pl.multiple_of(core * half, half), half)
        at = pl.ds(part * half, half)
        pair = []
        for which, (source, target) in enumerate(((keys_far, keys), (values_far, values))):
            copy = pltpu.make_async_copy(
                source.at[:, there], target.at[:, at], sems.at[part, which]
            )
            copy.start()
            pair.append(copy)
        copies.append(pair)
    for part, out in enumerate((other, mine)):
        for copy in copies[part]:
            copy.wait()
        for head in range(heads):
            at = columns(part * heads + head)
            out[head] = dot_tn(keys[:, at], values[:, at])


def within_kernel(
    queries_far, keys_far, values_far, grad_far, gain_far, after,
    within, upstream, queries, keys, values, grad, gain, sems,
):
    del after
    copies = [
        pltpu.make_async_copy(far, near, sems.at[at])
        for at, (far, near) in enumerate(
            (
                (queries_far, queries),
                (keys_far, keys),
                (values_far, values),
                (grad_far, grad),
                (gain_far, gain),
            )
        )
    ]
    for copy in copies:
        copy.start()
    mask = causal(queries.shape[0], False)
    for copy in copies:
        copy.wait()
    for head in range(queries.shape[1] // HEAD_DIM):
        at = columns(head)
        within[:, at] = dot_nn(scores(queries[:, at], keys[:, at], mask), values[:, at])
        upstream[:, at] = grad[:, at].astype(F32) * gain[:, at].astype(F32)


def split_kernel(mine, got, *pieces):
    for step, piece in enumerate(pieces):
        at = owner() ^ step
        piece[...] = mine[at] + got[at]


def join_kernel(count, *refs):
    total = refs[0][...]
    for ref in refs[1:count]:
        total = total + ref[...]
    refs[-1][...] = total


def members_kernel(reverse, group, rows, *refs):
    parts, refs = refs[:group], refs[group:]
    mirror, there, outs = refs[0], refs[1:rows], refs[rows:]
    row, low, high = here("row"), here("low"), here("high")
    ahead = jnp.where(before(1 - high, high, reverse), mirror[...], 0.0)
    for step in range(1, rows):
        sooner = before(row ^ step, row, reverse)
        ahead = ahead + jnp.where(sooner, there[step - 1][...], 0.0)
    for at, out in enumerate(outs):
        result = ahead
        for step in range(group):
            if step != at:
                sooner = before(low ^ step, low ^ at, reverse)
                result = result + jnp.where(sooner, parts[step][...], 0.0)
        out[...] = result


def merge_kernel(reverse, group, *refs):
    back, (mine, got, own, theirs) = refs[:group], refs[group:]
    first = before(here("core"), 1 - here("core"), reverse)
    for step in range(group):
        at = owner() ^ step
        own[at] = back[step][...] + jnp.where(first, 0.0, got[at])
        theirs[at] = back[step][...] + jnp.where(first, mine[at], 0.0)


def by_head(own, theirs, refs=False):
    half = own.shape[0]
    for part, states in enumerate((own, theirs)):
        core = 1 - here("core") if part else here("core")
        for at in range(half):
            head = core * half + at
            yield head, pl.ds(pl.multiple_of(head * HEAD_DIM, HEAD_DIM), HEAD_DIM), states.at[at] if refs else states[at]


def forward_kernel(queries, upstream, within, own, theirs, output, low, sums):
    tokens = queries.shape[0]
    square = jnp.zeros((tokens, HEAD_DIM), F32)
    mixed = jnp.zeros((tokens, HEAD_DIM), F32)
    for head, at, state in by_head(own, theirs):
        state_low = state.astype(BF16)
        low[head] = state_low
        out = within[:, at] + FACTOR * dot_nn(queries[:, at], state_low)
        output[:, at] = out
        square = square + out * out
        mixed = mixed + upstream[:, at] * out
    sums[0:1] = jnp.sum(square.T, axis=0, keepdims=True)
    sums[1:2] = jnp.sum(mixed.T, axis=0, keepdims=True)


def delta_kernel(queries, upstream, output, sums, sums_1, sums_2, sums_3, delta, mine, other):
    tokens = queries.shape[0]
    total = sums[...] + sums_1[...] + sums_2[...] + sums_3[...]
    inv_rms = lax.rsqrt(total[0:1] / FEATURES + EPSILON)
    pull = inv_rms * inv_rms * inv_rms * (total[1:2] / FEATURES)
    inv_rms = jnp.broadcast_to(inv_rms, (HEAD_DIM, tokens)).T
    pull = jnp.broadcast_to(pull, (HEAD_DIM, tokens)).T
    for head, at, back in by_head(mine, other, True):
        out_delta = (inv_rms * upstream[:, at] - pull * output[:, at]).astype(BF16)
        delta[:, at] = out_delta
        back[...] = dot_tn(out_delta, queries[:, at])


def query_kernel(keys, values, delta, low, after, query_grad):
    del after
    mask = causal(keys.shape[0], False)
    for head in range(low.shape[0]):
        at = columns(head)
        out_delta = delta[:, at]
        delta_scores = scores(out_delta, values[:, at], mask)
        grad = dot_nn(delta_scores, keys[:, at]) + FACTOR * dot_nt(out_delta, low[head])
        query_grad[:, at] = grad.astype(BF16)


def inner_kernel(queries, keys, values, delta, after, key_inner, value_inner):
    del after
    mask = causal(keys.shape[0], True)
    for head in range(queries.shape[1] // HEAD_DIM):
        at = columns(head)
        query, out_delta = queries[:, at], delta[:, at]
        key_inner[:, at] = dot_nn(scores(values[:, at], out_delta, mask), query)
        value_inner[:, at] = dot_nn(scores(keys[:, at], query, mask), out_delta)


def backward_kernel(keys, values, key_inner, value_inner, own, theirs, key_grad, value_grad):
    for _, at, state in by_head(own, theirs):
        later_low = state.astype(BF16)
        grad = key_inner[:, at] + FACTOR * dot_nn(values[:, at], later_low)
        key_grad[:, at] = grad.astype(BF16)
        grad = value_inner[:, at] + FACTOR * dot_nt(keys[:, at], later_low)
        value_grad[:, at] = grad.astype(BF16)


def swap(array, axis, distance):
    count = lax.axis_size(axis)
    return lax.ppermute(array, axis, [(at, at ^ distance) for at in range(count)])


def before(one, other, reverse):
    return one > other if reverse else one < other


def owner():
    return here("low") ^ ((lax.axis_size("low") - 1) * here("high"))


def entering(mine, other, reverse, beside):
    group, rows = lax.axis_size("low"), lax.axis_size("row")
    piece = near(mine.shape[1:])
    got = swap(other, "core", 1)
    parts = call(split_kernel, [piece] * group)(mine, got)
    made = beside(parts[0])
    parts = [parts[0]] + [swap(parts[step], "low", step) for step in range(1, group)]
    whole = call(functools.partial(join_kernel, group), piece)(*parts, *made)
    mirror = swap(whole, ("high", "low"), 2 * group - 1)
    whole = call(functools.partial(join_kernel, 2), piece)(whole, mirror)
    there = [swap(whole, "row", step) for step in range(1, rows)]
    back = call(functools.partial(members_kernel, reverse, group, rows), [piece] * group)(
        *parts, mirror, *there
    )
    back = [back[0]] + [swap(back[step], "low", step) for step in range(1, group)]
    half = near(mine.shape)
    own, theirs = call(functools.partial(merge_kernel, reverse, group), (half, half))(
        *back, mine, got
    )
    return own, swap(theirs, "core", 1), made


def on_device(queries, keys, values, out_grad, gain):
    tokens, width = queries.shape
    heads = width // HEAD_DIM
    gain = gain.reshape(1, width)
    wide = near((tokens, width), BF16)
    full = near((tokens, width))
    half = near((heads // 2, HEAD_DIM, HEAD_DIM))
    mine, other = call(
        totals_kernel,
        (half, half),
        far=2,
        scratch_shapes=[wide, wide, pltpu.SemaphoreType.DMA((2, 2))],
    )(keys, values)

    def beside_forward(after):
        return call(
            within_kernel,
            (full, full, wide, wide, wide),
            far=5,
            scratch_shapes=[wide, near((1, width), BF16), pltpu.SemaphoreType.DMA((5,))],
        )(queries, keys, values, out_grad, gain, after)

    own, theirs, (within, upstream, queries, keys, values) = entering(
        mine, other, False, beside_forward
    )
    output, low, sums = call(
        forward_kernel,
        (full, near((heads, HEAD_DIM, HEAD_DIM), BF16), near((2, tokens))),
    )(queries, upstream, within, own, theirs)
    others = [swap(sums, "head", step) for step in range(1, lax.axis_size("head"))]
    delta, mine, other = call(delta_kernel, (wide, half, half))(
        queries, upstream, output, sums, *others
    )

    def beside_backward(after):
        query_grad = call(query_kernel, wide)(keys, values, delta, low, after)
        inner = call(inner_kernel, (full, full))(queries, keys, values, delta, after)
        return query_grad, *inner

    own, theirs, (query_grad, key_inner, value_inner) = entering(
        mine, other, True, beside_backward
    )
    grads = jax.ShapeDtypeStruct((tokens, width), BF16)
    key_grad, value_grad = call(backward_kernel, (grads, grads))(
        keys, values, key_inner, value_inner, own, theirs
    )
    return query_grad, key_grad, value_grad


def solution(mesh):
    _, across = mesh.devices.shape
    shape = (4, 2, 4, 2, across)
    inner = Mesh(mesh.devices.reshape(shape), ("row", "high", "low", "core", "head"))
    spec = P(("row", "high", "low", "core"), "head")
    return jax.shard_map(
        on_device,
        mesh=inner,
        in_specs=(spec, spec, spec, spec, P("head")),
        out_specs=(spec, spec, spec),
        check_vma=False,
    )
```

```python
import functools

import jax
import jax.numpy as jnp
from jax import lax
from jax.experimental import pallas as pl
from jax.experimental.pallas import tpu as pltpu
from jax.sharding import Mesh
from jax.sharding import PartitionSpec as P

HEADS = 32
HEAD_DIM = 128
EPSILON = 1e-05
FEATURES = HEADS * HEAD_DIM
FACTOR = HEAD_DIM ** (-0.5)
F32 = jnp.float32
BF16 = jnp.bfloat16
VMEM_LIMIT = 16 * 1024 * 1024


def dot_nn(a, b):
    return lax.dot_general(a, b, (((1,), (0,)), ((), ())), preferred_element_type=F32)


def dot_nt(a, b):
    return lax.dot_general(a, b, (((1,), (1,)), ((), ())), preferred_element_type=F32)


def dot_tn(a, b):
    return lax.dot_general(a, b, (((0,), (0,)), ((), ())), preferred_element_type=F32)


def columns(head):
    return pl.ds(head * HEAD_DIM, HEAD_DIM)


def causal(count, transposed):
    row = lax.broadcasted_iota(jnp.int32, (count, count), 0)
    col = lax.broadcasted_iota(jnp.int32, (count, count), 1)
    return row <= col if transposed else col <= row


def scores(a, b, mask):
    return jnp.where(mask, dot_nt(a, b) * FACTOR, 0.0).astype(BF16)


def here(name):
    return lax.axis_index(name)


def near(shape, dtype=F32):
    return pltpu.VMEM(shape, dtype)


def call(kernel, out_shape, far=0, loose=0, **kwargs):
    def run(*operands):
        close = len(operands) - far - loose
        spaces = [pltpu.HBM] * far + [pltpu.VMEM] * close + [pl.ANY] * loose
        return pl.pallas_call(
            kernel,
            out_shape=out_shape,
            in_specs=[pl.BlockSpec(memory_space=space) for space in spaces],
            compiler_params=pltpu.CompilerParams(vmem_limit_bytes=VMEM_LIMIT),
            **kwargs,
        )(*map(pltpu.with_memory_space_constraint, operands, spaces))

    return run


def halves(far, near, sems):
    half = far.shape[1] // 2
    result = []
    for part in range(2):
        core = 1 - here("core") if part else here("core")
        there = pl.ds(pl.multiple_of(core * half, half), half)
        result.append((far.at[:, there], near.at[:, pl.ds(part * half, half)], sems.at[part]))
    return result


def fetch(far, near, sems):
    return [pltpu.make_async_copy(there, at, sem) for there, at, sem in halves(far, near, sems)]


def totals_kernel(part, keys_far, values_far, out, keys, values, sems):
    chunks = sems.shape[1]
    rows = keys.shape[0] // chunks
    half = keys.shape[1]
    core = 1 - here("core") if part else here("core")
    there = pl.ds(pl.multiple_of(core * half, half), half)
    copies = []
    for chunk in range(chunks):
        at = pl.ds(chunk * rows, rows)
        for which, (far, near) in enumerate(((keys_far, keys), (values_far, values))):
            copy = pltpu.make_async_copy(far.at[at, there], near.at[at], sems.at[which, chunk])
            copy.start()
            copies.append(copy)
    for copy in copies:
        copy.wait()
    for head in range(out.shape[0]):
        at = columns(head)
        out[head] = dot_tn(keys[:, at], values[:, at])


def within_kernel(
    queries_far, grad_far, gain_far, keys_0, keys_1, values_0, values_1, after,
    within, upstream, queries, grad, gain, sems,
):
    del after
    copies = [
        fetch(queries_far, queries, sems.at[0]),
        fetch(grad_far, grad, sems.at[1]),
        fetch(gain_far, gain, sems.at[2]),
    ]
    for pair in copies:
        for copy in pair:
            copy.start()
    mask = causal(queries.shape[0], False)
    for pair in copies:
        for copy in pair:
            copy.wait()
    heads = queries.shape[1] // HEAD_DIM // 2
    for part, (keys, values) in enumerate(((keys_0, values_0), (keys_1, values_1))):
        for head in range(heads):
            at, near = columns(part * heads + head), columns(head)
            within[:, at] = dot_nn(scores(queries[:, at], keys[:, near], mask), values[:, near])
            upstream[:, at] = grad[:, at].astype(F32) * gain[:, at].astype(F32)


def split_kernel(mine, got, *pieces):
    for step, piece in enumerate(pieces):
        at = owner() ^ step
        piece[...] = mine[at] + got[at]


def join_kernel(skip, count, *refs):
    parts = refs[skip : skip + count]
    total = parts[0][...]
    for part in parts[1:]:
        total = total + part[...]
    refs[-1][...] = total


def members_kernel(reverse, group, rows, *refs):
    parts, refs = refs[:group], refs[group:]
    mirror, there, outs = refs[0], refs[1:rows], refs[rows:]
    row, low, high = here("row"), here("low"), here("high")
    ahead = jnp.where(before(1 - high, high, reverse), mirror[...], 0.0)
    for step in range(1, rows):
        sooner = before(row ^ step, row, reverse)
        ahead = ahead + jnp.where(sooner, there[step - 1][...], 0.0)
    for at, out in enumerate(outs):
        result = ahead
        for step in range(group):
            if step != at:
                sooner = before(low ^ step, low ^ at, reverse)
                result = result + jnp.where(sooner, parts[step][...], 0.0)
        out[...] = result


def merge_kernel(reverse, group, *refs):
    back, (mine, got, own, theirs) = refs[:group], refs[group:]
    first = before(here("core"), 1 - here("core"), reverse)
    for step in range(group):
        at = owner() ^ step
        own[at] = back[step][...] + jnp.where(first, 0.0, got[at])
        theirs[at] = back[step][...] + jnp.where(first, mine[at], 0.0)


def forward_kernel(part, queries, upstream, within, state, *refs):
    before_sums, (output, low, sums) = refs[:part], refs[part:]
    heads = state.shape[0]
    tokens = queries.shape[0]
    square = jnp.zeros((tokens, HEAD_DIM), F32)
    mixed = jnp.zeros((tokens, HEAD_DIM), F32)
    for head in range(heads):
        at = columns(part * heads + head)
        state_low = state[head].astype(BF16)
        low[head] = state_low
        out = within[:, at] + FACTOR * dot_nn(queries[:, at], state_low)
        output[:, columns(head)] = out
        square = square + out * out
        mixed = mixed + upstream[:, at] * out
    for row, array in enumerate((square, mixed)):
        total = jnp.sum(array.T, axis=0, keepdims=True)
        for ref in before_sums:
            total = total + ref[row : row + 1]
        sums[row : row + 1] = total


def delta_kernel(part, queries, upstream, output, sums, sums_1, sums_2, sums_3, delta, back):
    tokens = queries.shape[0]
    heads = back.shape[0]
    total = sums[...] + sums_1[...] + sums_2[...] + sums_3[...]
    inv_rms = lax.rsqrt(total[0:1] / FEATURES + EPSILON)
    pull = inv_rms * inv_rms * inv_rms * (total[1:2] / FEATURES)
    inv_rms = jnp.broadcast_to(inv_rms, (HEAD_DIM, tokens)).T
    pull = jnp.broadcast_to(pull, (HEAD_DIM, tokens)).T
    for head in range(heads):
        at = columns(part * heads + head)
        out_delta = inv_rms * upstream[:, at] - pull * output[:, columns(head)]
        out_delta = out_delta.astype(BF16)
        delta[:, columns(head)] = out_delta
        back[head] = dot_tn(out_delta, queries[:, at])


def write(near, far, part, sem):
    half = near.shape[1]
    core = 1 - here("core") if part else here("core")
    there = pl.ds(pl.multiple_of(core * half, half), half)
    copy = pltpu.make_async_copy(near, far.at[:, there], sem)
    copy.start()
    return copy


def query_kernel(*refs):
    *operands, _, far, near_0, near_1, sems = refs
    mask = causal(operands[0].shape[0], False)
    copies = []
    for part, near in enumerate((near_0, near_1)):
        keys, values, delta, low = operands[part::2]
        for head in range(low.shape[0]):
            at = columns(head)
            out_delta = delta[:, at]
            delta_scores = scores(out_delta, values[:, at], mask)
            grad = dot_nn(delta_scores, keys[:, at]) + FACTOR * dot_nt(out_delta, low[head])
            near[:, at] = grad.astype(BF16)
        copies.append(write(near, far, part, sems.at[part]))
    for copy in copies:
        copy.wait()


def inner_kernel(part, queries, keys, values, delta, after, key_inner, value_inner):
    del after
    mask = causal(keys.shape[0], True)
    heads = delta.shape[1] // HEAD_DIM
    for head in range(heads):
        at = columns(head)
        query, out_delta = queries[:, columns(part * heads + head)], delta[:, at]
        key_inner[:, at] = dot_nn(scores(values[:, at], out_delta, mask), query)
        value_inner[:, at] = dot_nn(scores(keys[:, at], query, mask), out_delta)


def key_value_grads(keys, values, key_inner, value_inner, state, key_near, value_near):
    lows = [state[head].astype(BF16) for head in range(state.shape[0])]
    for head, later_low in enumerate(lows):
        at = columns(head)
        grad = key_inner[:, at] + FACTOR * dot_nn(values[:, at], later_low)
        key_near[:, at] = grad.astype(BF16)
    yield
    for head, later_low in enumerate(lows):
        at = columns(head)
        grad = value_inner[:, at] + FACTOR * dot_nt(keys[:, at], later_low)
        value_near[:, at] = grad.astype(BF16)
    yield


def backward_kernel(*refs):
    for _ in key_value_grads(*refs):
        pass


def last_kernel(
    keys, values, key_inner, value_inner, state, key_0, value_0,
    key_far, value_far, key_1, value_1, sems,
):
    copies = [
        write(key_0, key_far, 0, sems.at[0]),
        write(value_0, value_far, 0, sems.at[1]),
    ]
    steps = key_value_grads(keys, values, key_inner, value_inner, state, key_1, value_1)
    next(steps)
    copies.append(write(key_1, key_far, 1, sems.at[2]))
    next(steps)
    copies.append(write(value_1, value_far, 1, sems.at[3]))
    for copy in copies:
        copy.wait()


def swap(array, axis, distance):
    count = lax.axis_size(axis)
    return lax.ppermute(array, axis, [(at, at ^ distance) for at in range(count)])


def before(one, other, reverse):
    return one > other if reverse else one < other


def owner():
    return here("low") ^ (lax.axis_size("low") // 2 * here("high"))


def swaps(arrays, axis, order):
    there = {step: swap(arrays[step], axis, step) for step in order}
    return [there[step] for step in sorted(there)]


def entering(mine, other, reverse, beside):
    group, rows = lax.axis_size("low"), lax.axis_size("row")
    line, ring = (3, 2, 1), (1, 3, 2)
    piece = near(mine.shape[1:])
    got = swap(other, "core", 1)
    parts = call(split_kernel, [piece] * group)(mine, got)
    made = beside(parts[0])
    parts = [parts[0]] + swaps(parts, "low", line)
    first, *ties = made
    whole = call(functools.partial(join_kernel, int(reverse), group), piece, far=int(reverse))(
        *((first, *parts) if reverse else (*parts, first)), *ties
    )
    mirror = swap(whole, ("high", "low"), group + group // 2)
    whole = call(functools.partial(join_kernel, 0, 2), piece)(whole, mirror)
    there = swaps([whole] * rows, "row", ring)
    back = call(functools.partial(members_kernel, reverse, group, rows), [piece] * group)(
        *parts, mirror, *there
    )
    back = [back[0]] + swaps(back, "low", line)
    half = near(mine.shape)
    own, theirs = call(functools.partial(merge_kernel, reverse, group), (half, half))(
        *back, mine, got
    )
    return (own, swap(theirs, "core", 1)), made


def on_device(queries, keys, values, out_grad, gain):
    tokens, width = queries.shape
    heads = width // HEAD_DIM
    gain = gain.reshape(1, width)
    wide = near((tokens, width), BF16)
    full = near((tokens, width))
    half = near((heads // 2, HEAD_DIM, HEAD_DIM))
    half_low = near(half.shape, BF16)
    half_wide = near((tokens, width // 2), BF16)
    half_full = near((tokens, width // 2))
    sums_shape = near((2, tokens))
    grads = pltpu.HBM((tokens, width), BF16)
    other, mine = (
        call(
            functools.partial(totals_kernel, part),
            (half, half_wide, half_wide),
            far=2,
            scratch_shapes=[pltpu.SemaphoreType.DMA((2, 4))],
        )(keys, values)
        for part in (1, 0)
    )
    mine, *near_0 = mine
    other, *near_1 = other
    keys, values = zip(near_0, near_1)

    def beside_forward(after):
        return call(
            within_kernel,
            (full, full, wide),
            far=3,
            scratch_shapes=[wide, near((1, width), BF16), pltpu.SemaphoreType.DMA((3, 2))],
        )(queries, out_grad, gain, *keys, *values, after)

    states, (within, upstream, queries) = entering(mine, other, False, beside_forward)
    outputs, lows, sums = [], [], []
    for part, state in enumerate(states):
        output, low, *sums = call(
            functools.partial(forward_kernel, part), (half_full, half_low, sums_shape)
        )(queries, upstream, within, state, *sums)
        outputs.append(output)
        lows.append(low)
    sums = swaps(sums * lax.axis_size("head"), "head", (1, 3, 2)) + sums
    deltas, backs = zip(
        *(
            call(functools.partial(delta_kernel, part), (half_wide, half))(
                queries, upstream, outputs[part], *sums
            )
            for part in (1, 0)
        )
    )
    deltas, backs = deltas[::-1], backs[::-1]

    def beside_backward(after):
        query_grad = call(
            query_kernel,
            grads,
            scratch_shapes=[half_wide, half_wide, pltpu.SemaphoreType.DMA((2,))],
        )(*keys, *values, *deltas, *lows, after)
        inner = [
            call(functools.partial(inner_kernel, part), (half_full, half_full))(
                queries, keys[part], values[part], deltas[part], after
            )
            for part in range(2)
        ]
        return query_grad, *inner[0], *inner[1]

    states, (query_grad, *inner) = entering(*backs, True, beside_backward)
    key_0, value_0 = call(backward_kernel, (half_wide, half_wide))(
        keys[0], values[0], *inner[:2], states[0]
    )
    key_grad, value_grad = call(
        last_kernel,
        (grads, grads),
        scratch_shapes=[half_wide, half_wide, pltpu.SemaphoreType.DMA((4,))],
    )(keys[1], values[1], *inner[2:], states[1], key_0, value_0)
    return query_grad, key_grad, value_grad


def solution(mesh):
    _, across = mesh.devices.shape
    shape = (4, 2, 4, 2, across)
    inner = Mesh(mesh.devices.reshape(shape), ("row", "high", "low", "core", "head"))
    spec = P(("row", "high", "low", "core"), "head")
    return jax.shard_map(
        on_device,
        mesh=inner,
        in_specs=(spec, spec, spec, spec, P("head")),
        out_specs=(spec, spec, spec),
        check_vma=False,
    )
```

```python
import functools

import jax
import jax.numpy as jnp
from jax import lax
from jax.experimental import pallas as pl
from jax.experimental.pallas import tpu as pltpu
from jax.sharding import Mesh
from jax.sharding import PartitionSpec as P

HEADS = 32
HEAD_DIM = 128
BLOCK = 128
EPSILON = 1e-05
FEATURES = HEADS * HEAD_DIM
FACTOR = HEAD_DIM ** (-0.5)
F32 = jnp.float32
BF16 = jnp.bfloat16
VMEM_LIMIT = 16 * 1024 * 1024


def dot_nn(a, b):
    return lax.dot_general(a, b, (((1,), (0,)), ((), ())), preferred_element_type=F32)


def dot_nt(a, b):
    return lax.dot_general(a, b, (((1,), (1,)), ((), ())), preferred_element_type=F32)


def dot_tn(a, b):
    return lax.dot_general(a, b, (((0,), (0,)), ((), ())), preferred_element_type=F32)


def columns(head):
    return pl.ds(head * HEAD_DIM, HEAD_DIM)


def blocks(tokens):
    return [slice(at, at + BLOCK) for at in range(0, tokens, BLOCK)]


def causal(count, transposed):
    row = lax.broadcasted_iota(jnp.int32, (count, count), 0)
    col = lax.broadcasted_iota(jnp.int32, (count, count), 1)
    order = row <= col if transposed else col <= row
    return order & (row // BLOCK == col // BLOCK)


def scores(a, b, mask):
    return jnp.where(mask, dot_nt(a, b) * FACTOR, 0.0).astype(BF16)


def here(name):
    return lax.axis_index(name)


def near(shape, dtype=F32):
    return pltpu.VMEM(shape, dtype)


def call(kernel, out_shape, far=0, loose=0, **kwargs):
    def run(*operands):
        close = len(operands) - far - loose
        spaces = [pltpu.HBM] * far + [pltpu.VMEM] * close + [pl.ANY] * loose
        return pl.pallas_call(
            kernel,
            out_shape=out_shape,
            in_specs=[pl.BlockSpec(memory_space=space) for space in spaces],
            compiler_params=pltpu.CompilerParams(vmem_limit_bytes=VMEM_LIMIT),
            **kwargs,
        )(*map(pltpu.with_memory_space_constraint, operands, spaces))

    return run


def halves(far, near, sems):
    half = far.shape[1] // 2
    result = []
    for part in range(2):
        core = 1 - here("core") if part else here("core")
        there = pl.ds(pl.multiple_of(core * half, half), half)
        result.append((far.at[:, there], near.at[:, pl.ds(part * half, half)], sems.at[part]))
    return result


def fetch(far, near, sems):
    return [pltpu.make_async_copy(there, at, sem) for there, at, sem in halves(far, near, sems)]


def totals_kernel(part, keys_far, values_far, out, sooner, keys, values, sems):
    chunks = sems.shape[1]
    rows = keys.shape[0] // chunks
    half = keys.shape[1]
    core = 1 - here("core") if part else here("core")
    there = pl.ds(pl.multiple_of(core * half, half), half)
    copies = []
    for chunk in range(chunks):
        at = pl.ds(chunk * rows, rows)
        for which, (far, near) in enumerate(((keys_far, keys), (values_far, values))):
            copy = pltpu.make_async_copy(far.at[at, there], near.at[at], sems.at[which, chunk])
            copy.start()
            copies.append(copy)
    for copy in copies:
        copy.wait()
    for head in range(out.shape[0]):
        at = columns(head)
        total = jnp.zeros(out.shape[1:], F32)
        for block, rows in enumerate(blocks(keys.shape[0])):
            if block:
                sooner[head, block - 1] = total
            total = total + dot_tn(keys[rows, at], values[rows, at])
        out[head] = total


def within_kernel(
    queries_far, grad_far, gain_far, keys_0, keys_1, values_0, values_1, after,
    within, upstream, queries, grad, gain, sems,
):
    del after
    copies = [
        fetch(queries_far, queries, sems.at[0]),
        fetch(grad_far, grad, sems.at[1]),
        fetch(gain_far, gain, sems.at[2]),
    ]
    for pair in copies:
        for copy in pair:
            copy.start()
    mask = causal(queries.shape[0], False)
    for pair in copies:
        for copy in pair:
            copy.wait()
    heads = queries.shape[1] // HEAD_DIM // 2
    for part, (keys, values) in enumerate(((keys_0, values_0), (keys_1, values_1))):
        for head in range(heads):
            at, near = columns(part * heads + head), columns(head)
            within[:, at] = dot_nn(scores(queries[:, at], keys[:, near], mask), values[:, near])
            upstream[:, at] = grad[:, at].astype(F32) * gain[:, at].astype(F32)


def split_kernel(mine, got, *pieces):
    for step, piece in enumerate(pieces):
        at = owner() ^ step
        piece[...] = mine[at] + got[at]


def join_kernel(skip, count, *refs):
    parts = refs[skip : skip + count]
    total = parts[0][...]
    for part in parts[1:]:
        total = total + part[...]
    refs[-1][...] = total


def members_kernel(reverse, group, rows, *refs):
    parts, refs = refs[:group], refs[group:]
    mirror, there, outs = refs[0], refs[1:rows], refs[rows:]
    row, low, high = here("row"), here("low"), here("high")
    ahead = jnp.where(before(1 - high, high, reverse), mirror[...], 0.0)
    for step in range(1, rows):
        sooner = before(row ^ step, row, reverse)
        ahead = ahead + jnp.where(sooner, there[step - 1][...], 0.0)
    for at, out in enumerate(outs):
        result = ahead
        for step in range(group):
            if step != at:
                sooner = before(low ^ step, low ^ at, reverse)
                result = result + jnp.where(sooner, parts[step][...], 0.0)
        out[...] = result


def merge_kernel(reverse, group, *refs):
    back, (mine, got, own, theirs) = refs[:group], refs[group:]
    first = before(here("core"), 1 - here("core"), reverse)
    for step in range(group):
        at = owner() ^ step
        own[at] = back[step][...] + jnp.where(first, 0.0, got[at])
        theirs[at] = back[step][...] + jnp.where(first, mine[at], 0.0)


def forward_kernel(part, queries, upstream, within, state, sooner, *refs):
    before_sums, (output, low, sums) = refs[:part], refs[part:]
    heads = state.shape[0]
    tokens = queries.shape[0]
    square = jnp.zeros((tokens, HEAD_DIM), F32)
    mixed = jnp.zeros((tokens, HEAD_DIM), F32)
    for head in range(heads):
        at = columns(part * heads + head)
        carried = []
        for block, rows in enumerate(blocks(tokens)):
            wide = state[head]
            if block:
                wide = wide + sooner[head, block - 1]
            state_low = wide.astype(BF16)
            low[head, block] = state_low
            carried.append(dot_nn(queries[rows, at], state_low))
        out = within[:, at] + FACTOR * jnp.concatenate(carried)
        output[:, columns(head)] = out
        square = square + out * out
        mixed = mixed + upstream[:, at] * out
    for row, array in enumerate((square, mixed)):
        total = jnp.sum(array.T, axis=0, keepdims=True)
        for ref in before_sums:
            total = total + ref[row : row + 1]
        sums[row : row + 1] = total


def delta_kernel(part, queries, upstream, output, sums, sums_1, sums_2, sums_3, delta, back, later):
    tokens = queries.shape[0]
    heads = back.shape[0]
    total = sums[...] + sums_1[...] + sums_2[...] + sums_3[...]
    inv_rms = lax.rsqrt(total[0:1] / FEATURES + EPSILON)
    pull = inv_rms * inv_rms * inv_rms * (total[1:2] / FEATURES)
    inv_rms = jnp.broadcast_to(inv_rms, (HEAD_DIM, tokens)).T
    pull = jnp.broadcast_to(pull, (HEAD_DIM, tokens)).T
    for head in range(heads):
        at = columns(part * heads + head)
        out_delta = inv_rms * upstream[:, at] - pull * output[:, columns(head)]
        out_delta = out_delta.astype(BF16)
        delta[:, columns(head)] = out_delta
        total = jnp.zeros(back.shape[1:], F32)
        parts = blocks(tokens)
        for block in reversed(range(len(parts))):
            rows = parts[block]
            if block + 1 < len(parts):
                later[head, block] = total
            total = total + dot_tn(out_delta[rows], queries[rows, at])
        back[head] = total


def write(near, far, part, sem):
    half = near.shape[1]
    core = 1 - here("core") if part else here("core")
    there = pl.ds(pl.multiple_of(core * half, half), half)
    copy = pltpu.make_async_copy(near, far.at[:, there], sem)
    copy.start()
    return copy


def query_kernel(*refs):
    *operands, _, far, near_0, near_1, sems = refs
    mask = causal(operands[0].shape[0], False)
    copies = []
    for part, near in enumerate((near_0, near_1)):
        keys, values, delta, low = operands[part::2]
        for head in range(low.shape[0]):
            at = columns(head)
            out_delta = delta[:, at]
            carried = [
                dot_nt(delta[rows, at], low[head, block])
                for block, rows in enumerate(blocks(keys.shape[0]))
            ]
            delta_scores = scores(out_delta, values[:, at], mask)
            grad = dot_nn(delta_scores, keys[:, at]) + FACTOR * jnp.concatenate(carried)
            near[:, at] = grad.astype(BF16)
        copies.append(write(near, far, part, sems.at[part]))
    for copy in copies:
        copy.wait()


def inner_kernel(part, queries, keys, values, delta, after, key_inner, value_inner):
    del after
    mask = causal(keys.shape[0], True)
    heads = delta.shape[1] // HEAD_DIM
    for head in range(heads):
        at = columns(head)
        query, out_delta = queries[:, columns(part * heads + head)], delta[:, at]
        key_inner[:, at] = dot_nn(scores(values[:, at], out_delta, mask), query)
        value_inner[:, at] = dot_nn(scores(keys[:, at], query, mask), out_delta)


def key_value_grads(keys, values, key_inner, value_inner, state, later, key_near, value_near):
    parts = blocks(keys.shape[0])
    heads = range(state.shape[0])
    lows = {}
    for head in heads:
        for block in range(len(parts)):
            wide = state[head]
            if block + 1 < len(parts):
                wide = wide + later[head, block]
            lows[head, block] = wide.astype(BF16)
    for head in heads:
        at = columns(head)
        carried = [dot_nn(values[rows, at], lows[head, n]) for n, rows in enumerate(parts)]
        grad = key_inner[:, at] + FACTOR * jnp.concatenate(carried)
        key_near[:, at] = grad.astype(BF16)
    yield
    for head in heads:
        at = columns(head)
        carried = [dot_nt(keys[rows, at], lows[head, n]) for n, rows in enumerate(parts)]
        grad = value_inner[:, at] + FACTOR * jnp.concatenate(carried)
        value_near[:, at] = grad.astype(BF16)
    yield


def backward_kernel(*refs):
    for _ in key_value_grads(*refs):
        pass


def last_kernel(
    keys, values, key_inner, value_inner, state, later, key_0, value_0,
    key_far, value_far, key_1, value_1, sems,
):
    copies = [
        write(key_0, key_far, 0, sems.at[0]),
        write(value_0, value_far, 0, sems.at[1]),
    ]
    steps = key_value_grads(
        keys, values, key_inner, value_inner, state, later, key_1, value_1
    )
    next(steps)
    copies.append(write(key_1, key_far, 1, sems.at[2]))
    next(steps)
    copies.append(write(value_1, value_far, 1, sems.at[3]))
    for copy in copies:
        copy.wait()


def swap(array, axis, distance):
    count = lax.axis_size(axis)
    return lax.ppermute(array, axis, [(at, at ^ distance) for at in range(count)])


def before(one, other, reverse):
    return one > other if reverse else one < other


def owner():
    return here("low") ^ (lax.axis_size("low") // 2 * here("high"))


def swaps(arrays, axis, order):
    there = {step: swap(arrays[step], axis, step) for step in order}
    return [there[step] for step in sorted(there)]


def entering(mine, other, reverse, beside):
    group, rows = lax.axis_size("low"), lax.axis_size("row")
    line, ring = (3, 2, 1), (1, 3, 2)
    piece = near(mine.shape[1:])
    got = swap(other, "core", 1)
    parts = call(split_kernel, [piece] * group)(mine, got)
    made = beside(parts[0])
    parts = [parts[0]] + swaps(parts, "low", line)
    first, *ties = made
    whole = call(functools.partial(join_kernel, int(reverse), group), piece, far=int(reverse))(
        *((first, *parts) if reverse else (*parts, first)), *ties
    )
    mirror = swap(whole, ("high", "low"), group + group // 2)
    whole = call(functools.partial(join_kernel, 0, 2), piece)(whole, mirror)
    there = swaps([whole] * rows, "row", ring)
    back = call(functools.partial(members_kernel, reverse, group, rows), [piece] * group)(
        *parts, mirror, *there
    )
    back = [back[0]] + swaps(back, "low", line)
    half = near(mine.shape)
    own, theirs = call(functools.partial(merge_kernel, reverse, group), (half, half))(
        *back, mine, got
    )
    return (own, swap(theirs, "core", 1)), made


def on_device(queries, keys, values, out_grad, gain):
    tokens, width = queries.shape
    heads = width // HEAD_DIM
    gain = gain.reshape(1, width)
    wide = near((tokens, width), BF16)
    full = near((tokens, width))
    half = near((heads // 2, HEAD_DIM, HEAD_DIM))
    inner_blocks = near((heads // 2, tokens // BLOCK - 1, HEAD_DIM, HEAD_DIM))
    half_low = near((heads // 2, tokens // BLOCK, HEAD_DIM, HEAD_DIM), BF16)
    half_wide = near((tokens, width // 2), BF16)
    half_full = near((tokens, width // 2))
    sums_shape = near((2, tokens))
    grads = pltpu.HBM((tokens, width), BF16)
    other, mine = (
        call(
            functools.partial(totals_kernel, part),
            (half, inner_blocks, half_wide, half_wide),
            far=2,
            scratch_shapes=[pltpu.SemaphoreType.DMA((2, 4))],
        )(keys, values)
        for part in (1, 0)
    )
    mine, sooner_0, *near_0 = mine
    other, sooner_1, *near_1 = other
    sooner = sooner_0, sooner_1
    keys, values = zip(near_0, near_1)

    def beside_forward(after):
        return call(
            within_kernel,
            (full, full, wide),
            far=3,
            scratch_shapes=[wide, near((1, width), BF16), pltpu.SemaphoreType.DMA((3, 2))],
        )(queries, out_grad, gain, *keys, *values, after)

    states, (within, upstream, queries) = entering(mine, other, False, beside_forward)
    outputs, lows, sums = [], [], []
    for part, state in enumerate(states):
        output, low, *sums = call(
            functools.partial(forward_kernel, part), (half_full, half_low, sums_shape)
        )(queries, upstream, within, state, sooner[part], *sums)
        outputs.append(output)
        lows.append(low)
    sums = swaps(sums * lax.axis_size("head"), "head", (1, 3, 2)) + sums
    deltas, backs, later = zip(
        *(
            call(functools.partial(delta_kernel, part), (half_wide, half, inner_blocks))(
                queries, upstream, outputs[part], *sums
            )
            for part in (1, 0)
        )
    )
    deltas, backs, later = deltas[::-1], backs[::-1], later[::-1]

    def beside_backward(after):
        query_grad = call(
            query_kernel,
            grads,
            scratch_shapes=[half_wide, half_wide, pltpu.SemaphoreType.DMA((2,))],
        )(*keys, *values, *deltas, *lows, after)
        inner = [
            call(functools.partial(inner_kernel, part), (half_full, half_full))(
                queries, keys[part], values[part], deltas[part], after
            )
            for part in range(2)
        ]
        return query_grad, *inner[0], *inner[1]

    states, (query_grad, *inner) = entering(*backs, True, beside_backward)
    key_0, value_0 = call(backward_kernel, (half_wide, half_wide))(
        keys[0], values[0], *inner[:2], states[0], later[0]
    )
    key_grad, value_grad = call(
        last_kernel,
        (grads, grads),
        scratch_shapes=[half_wide, half_wide, pltpu.SemaphoreType.DMA((4,))],
    )(keys[1], values[1], *inner[2:], states[1], later[1], key_0, value_0)
    return query_grad, key_grad, value_grad


def solution(mesh):
    _, across = mesh.devices.shape
    shape = (4, 2, 4, 2, across)
    inner = Mesh(mesh.devices.reshape(shape), ("row", "high", "low", "core", "head"))
    spec = P(("row", "high", "low", "core"), "head")
    return jax.shard_map(
        on_device,
        mesh=inner,
        in_specs=(spec, spec, spec, spec, P("head")),
        out_specs=(spec, spec, spec),
        check_vma=False,
    )
```

```python
import functools

import jax
import jax.numpy as jnp
from jax import lax
from jax.experimental import pallas as pl
from jax.experimental.pallas import tpu as pltpu
from jax.sharding import Mesh
from jax.sharding import PartitionSpec as P

HEADS = 32
HEAD_DIM = 128
BLOCK = 128
EPSILON = 1e-05
FEATURES = HEADS * HEAD_DIM
FACTOR = HEAD_DIM ** (-0.5)
F32 = jnp.float32
BF16 = jnp.bfloat16
VMEM_LIMIT = 16 * 1024 * 1024
STEPS = ((3,), (2, 1, 0))


def dot_nn(a, b):
    return lax.dot_general(a, b, (((1,), (0,)), ((), ())), preferred_element_type=F32)


def dot_nt(a, b):
    return lax.dot_general(a, b, (((1,), (1,)), ((), ())), preferred_element_type=F32)


def dot_tn(a, b):
    return lax.dot_general(a, b, (((0,), (0,)), ((), ())), preferred_element_type=F32)


def columns(head):
    return pl.ds(head * HEAD_DIM, HEAD_DIM)


def columns_of(part, step, heads):
    head = part * heads + (owner() ^ step)
    return pl.ds(pl.multiple_of(head * HEAD_DIM, HEAD_DIM), HEAD_DIM)


def blocks(tokens):
    return [slice(at, at + BLOCK) for at in range(0, tokens, BLOCK)]


def causal(count, transposed):
    row = lax.broadcasted_iota(jnp.int32, (count, count), 0)
    col = lax.broadcasted_iota(jnp.int32, (count, count), 1)
    order = row <= col if transposed else col <= row
    return order & (row // BLOCK == col // BLOCK)


def scores(a, b, mask):
    return jnp.where(mask, dot_nt(a, b) * FACTOR, 0.0).astype(BF16)


def here(name):
    return lax.axis_index(name)


def near(shape, dtype=F32):
    return pltpu.VMEM(shape, dtype)


def call(kernel, out_shape, far=0, loose=0, **kwargs):
    def run(*operands):
        close = len(operands) - far - loose
        spaces = [pltpu.HBM] * far + [pltpu.VMEM] * close + [pl.ANY] * loose
        return pl.pallas_call(
            kernel,
            out_shape=out_shape,
            in_specs=[pl.BlockSpec(memory_space=space) for space in spaces],
            compiler_params=pltpu.CompilerParams(vmem_limit_bytes=VMEM_LIMIT),
            **kwargs,
        )(*map(pltpu.with_memory_space_constraint, operands, spaces))

    return run


def halves(far, near, sems):
    half = far.shape[1] // 2
    result = []
    for part in range(2):
        core = 1 - here("core") if part else here("core")
        there = pl.ds(pl.multiple_of(core * half, half), half)
        result.append((far.at[:, there], near.at[:, pl.ds(part * half, half)], sems.at[part]))
    return result


def fetch(far, near, sems):
    return [pltpu.make_async_copy(there, at, sem) for there, at, sem in halves(far, near, sems)]


def key_value_states(keys, values, first, rest, sooner):
    heads = keys.shape[1] // HEAD_DIM
    for out, steps in zip((first, rest), STEPS):
        for index, step in enumerate(steps):
            at = columns_of(0, step, heads)
            total = jnp.zeros(out.shape[1:], F32)
            for block, rows in enumerate(blocks(keys.shape[0])):
                if block:
                    sooner[owner() ^ step, block - 1] = total
                total = total + dot_tn(keys[rows, at], values[rows, at])
            out[index] = total


def other_totals_kernel(
    keys_far, values_far, first, rest, sooner, keys_0, keys_1, values_0, values_1, sems
):
    chunks = sems.shape[2]
    rows = keys_0.shape[0] // chunks
    half = keys_0.shape[1]
    copies = []
    for part, arrays in ((1, (keys_1, values_1)), (0, (keys_0, values_0))):
        core = 1 - here("core") if part else here("core")
        there = pl.ds(pl.multiple_of(core * half, half), half)
        group = []
        for which, (far, near) in enumerate(zip((keys_far, values_far), arrays)):
            for chunk in range(chunks):
                at = pl.ds(chunk * rows, rows)
                copy = pltpu.make_async_copy(
                    far.at[at, there], near.at[at], sems.at[part, which, chunk]
                )
                copy.start()
                group.append(copy)
        copies.append(group)
    for copy in copies[0]:
        copy.wait()
    key_value_states(keys_1, values_1, first, rest, sooner)
    for copy in copies[1]:
        copy.wait()


def within_kernel(
    queries_far, grad_far, gain_far, keys_0, keys_1, values_0, values_1, after,
    within, upstream, queries, grad, gain, sems,
):
    del after
    copies = [
        fetch(queries_far, queries, sems.at[0]),
        fetch(grad_far, grad, sems.at[1]),
        fetch(gain_far, gain, sems.at[2]),
    ]
    for pair in copies:
        for copy in pair:
            copy.start()
    mask = causal(queries.shape[0], False)
    for pair in copies:
        for copy in pair:
            copy.wait()
    heads = queries.shape[1] // HEAD_DIM // 2
    for part, (keys, values) in enumerate(((keys_0, values_0), (keys_1, values_1))):
        for head in range(heads):
            at, near = columns(part * heads + head), columns(head)
            within[:, at] = dot_nn(scores(queries[:, at], keys[:, near], mask), values[:, near])
            upstream[:, at] = grad[:, at].astype(F32) * gain[:, at].astype(F32)


def split_kernel(mine, got, *pieces):
    for index, piece in enumerate(pieces):
        piece[...] = mine[index] + got[index]


def join_kernel(skip, count, *refs):
    parts = refs[skip : skip + count]
    total = parts[0][...]
    for part in parts[1:]:
        total = total + part[...]
    refs[-1][...] = total


def members_kernel(reverse, group, rows, *refs):
    parts, refs = refs[:group], refs[group:]
    mirror, there, outs = refs[0], refs[1:rows], refs[rows:]
    row, low, high = here("row"), here("low"), here("high")
    ahead = jnp.where(before(1 - high, high, reverse), mirror[...], 0.0)
    for step in range(1, rows):
        sooner = before(row ^ step, row, reverse)
        ahead = ahead + jnp.where(sooner, there[step - 1][...], 0.0)
    for at, out in enumerate(outs):
        result = ahead
        for step in range(group):
            if step != at:
                sooner = before(low ^ step, low ^ at, reverse)
                result = result + jnp.where(sooner, parts[step][...], 0.0)
        out[...] = result


def merge_kernel(reverse, *refs):
    *back, mine_0, mine_1, got_0, got_1, own, theirs = refs
    first = before(here("core"), 1 - here("core"), reverse)
    for mine, got, steps in ((mine_0, got_0, STEPS[0]), (mine_1, got_1, STEPS[1])):
        for index, step in enumerate(steps):
            at = owner() ^ step
            own[at] = back[step][...] + jnp.where(first, 0.0, got[index])
            theirs[at] = back[step][...] + jnp.where(first, mine[index], 0.0)


def forward_kernel(part, queries, upstream, within, state, sooner, *refs):
    before_sums, (output, low, sums) = refs[:part], refs[part:]
    heads = state.shape[0]
    tokens = queries.shape[0]
    square = jnp.zeros((tokens, HEAD_DIM), F32)
    mixed = jnp.zeros((tokens, HEAD_DIM), F32)
    for head in range(heads):
        at = columns(part * heads + head)
        carried = []
        for block, rows in enumerate(blocks(tokens)):
            wide = state[head]
            if block:
                wide = wide + sooner[head, block - 1]
            state_low = wide.astype(BF16)
            low[head, block] = state_low
            carried.append(dot_nn(queries[rows, at], state_low))
        out = within[:, at] + FACTOR * jnp.concatenate(carried)
        output[:, columns(head)] = out
        square = square + out * out
        mixed = mixed + upstream[:, at] * out
    for row, array in enumerate((square, mixed)):
        total = jnp.sum(array.T, axis=0, keepdims=True)
        for ref in before_sums:
            total = total + ref[row : row + 1]
        sums[row : row + 1] = total


def delta_kernel(part, queries, upstream, output, *refs):
    sums, (delta, first, rest, later) = refs[:4], refs[4:]
    tokens = queries.shape[0]
    heads = delta.shape[1] // HEAD_DIM
    total = sums[0][...] + sums[1][...] + sums[2][...] + sums[3][...]
    inv_rms = lax.rsqrt(total[0:1] / FEATURES + EPSILON)
    pull = inv_rms * inv_rms * inv_rms * (total[1:2] / FEATURES)
    inv_rms = jnp.broadcast_to(inv_rms, (HEAD_DIM, tokens)).T
    pull = jnp.broadcast_to(pull, (HEAD_DIM, tokens)).T
    for back, steps in zip((first, rest), STEPS):
        for index, step in enumerate(steps):
            at, near = columns_of(part, step, heads), columns_of(0, step, heads)
            out_delta = (inv_rms * upstream[:, at] - pull * output[:, near]).astype(BF16)
            delta[:, near] = out_delta
            total = jnp.zeros(back.shape[1:], F32)
            parts = blocks(tokens)
            for block in reversed(range(len(parts))):
                rows = parts[block]
                if block + 1 < len(parts):
                    later[owner() ^ step, block] = total
                total = total + dot_tn(out_delta[rows], queries[rows, at])
            back[index] = total


def write(near, far, part, sem):
    half = near.shape[1]
    core = 1 - here("core") if part else here("core")
    there = pl.ds(pl.multiple_of(core * half, half), half)
    copy = pltpu.make_async_copy(near, far.at[:, there], sem)
    copy.start()
    return copy


def query_kernel(*refs):
    *operands, _, far, near_0, near_1, sems = refs
    mask = causal(operands[0].shape[0], False)
    copies = []
    for part, near in enumerate((near_0, near_1)):
        keys, values, delta, low = operands[part::2]
        for head in range(low.shape[0]):
            at = columns(head)
            out_delta = delta[:, at]
            carried = [
                dot_nt(delta[rows, at], low[head, block])
                for block, rows in enumerate(blocks(keys.shape[0]))
            ]
            delta_scores = scores(out_delta, values[:, at], mask)
            grad = dot_nn(delta_scores, keys[:, at]) + FACTOR * jnp.concatenate(carried)
            near[:, at] = grad.astype(BF16)
        copies.append(write(near, far, part, sems.at[part]))
    for copy in copies:
        copy.wait()


def inner_kernel(part, queries, keys, values, delta, after, key_inner, value_inner):
    del after
    mask = causal(keys.shape[0], True)
    heads = delta.shape[1] // HEAD_DIM
    for head in range(heads):
        at = columns(head)
        query, out_delta = queries[:, columns(part * heads + head)], delta[:, at]
        key_inner[:, at] = dot_nn(scores(values[:, at], out_delta, mask), query)
        value_inner[:, at] = dot_nn(scores(keys[:, at], query, mask), out_delta)


def key_value_grads(keys, values, key_inner, value_inner, state, later, key_near, value_near):
    parts = blocks(keys.shape[0])
    heads = range(state.shape[0])
    lows = {}
    for head in heads:
        for block in range(len(parts)):
            wide = state[head]
            if block + 1 < len(parts):
                wide = wide + later[head, block]
            lows[head, block] = wide.astype(BF16)
    for head in heads:
        at = columns(head)
        carried = [dot_nn(values[rows, at], lows[head, n]) for n, rows in enumerate(parts)]
        grad = key_inner[:, at] + FACTOR * jnp.concatenate(carried)
        key_near[:, at] = grad.astype(BF16)
    yield
    for head in heads:
        at = columns(head)
        carried = [dot_nt(keys[rows, at], lows[head, n]) for n, rows in enumerate(parts)]
        grad = value_inner[:, at] + FACTOR * jnp.concatenate(carried)
        value_near[:, at] = grad.astype(BF16)
    yield


def backward_kernel(*refs):
    for _ in key_value_grads(*refs):
        pass


def last_kernel(
    keys, values, key_inner, value_inner, state, later, key_0, value_0,
    key_far, value_far, key_1, value_1, sems,
):
    copies = [
        write(key_0, key_far, 0, sems.at[0]),
        write(value_0, value_far, 0, sems.at[1]),
    ]
    steps = key_value_grads(
        keys, values, key_inner, value_inner, state, later, key_1, value_1
    )
    next(steps)
    copies.append(write(key_1, key_far, 1, sems.at[2]))
    next(steps)
    copies.append(write(value_1, value_far, 1, sems.at[3]))
    for copy in copies:
        copy.wait()


def swap(array, axis, distance):
    count = lax.axis_size(axis)
    return lax.ppermute(array, axis, [(at, at ^ distance) for at in range(count)])


def before(one, other, reverse):
    return one > other if reverse else one < other


def owner():
    return here("low") ^ (lax.axis_size("low") // 2 * here("high"))


def swaps(arrays, axis, order):
    there = {step: swap(arrays[step], axis, step) for step in order}
    return [there[step] for step in sorted(there)]


def entering(mine, other, reverse, beside_first, beside_second):
    group, rows = lax.axis_size("low"), lax.axis_size("row")
    line, ring = (3, 2, 1), (1, 3, 2)
    piece = near(mine[0].shape[1:])
    got = [swap(array, "core", 1) for array in other]
    parts = {}
    for steps, *arrays in zip(STEPS, mine, got):
        parts.update(zip(steps, call(split_kernel, [piece] * len(steps))(*arrays)))
    made = beside_first(parts[0])
    parts = [parts[0]] + swaps(parts, "low", line)
    whole = call(functools.partial(join_kernel, 0, group), piece)(*parts, *made)
    second = beside_second(whole)
    mirror = swap(whole, ("high", "low"), group + group // 2)
    far = len(second)
    whole = call(functools.partial(join_kernel, far, 2), piece, far=far)(*second, whole, mirror)
    there = swaps([whole] * rows, "row", ring)
    back = call(functools.partial(members_kernel, reverse, group, rows), [piece] * group)(
        *parts, mirror, *there
    )
    back = [back[0]] + swaps(back, "low", line)
    half = near((group * mine[0].shape[0], *mine[0].shape[1:]))
    own, theirs = call(functools.partial(merge_kernel, reverse), (half, half))(
        *back, *mine, *got
    )
    return (own, swap(theirs, "core", 1)), made, second


def on_device(queries, keys, values, out_grad, gain):
    tokens, width = queries.shape
    heads = width // HEAD_DIM
    gain = gain.reshape(1, width)
    wide = near((tokens, width), BF16)
    full = near((tokens, width))
    half = near((heads // 2, HEAD_DIM, HEAD_DIM))
    inner_blocks = near((heads // 2, tokens // BLOCK - 1, HEAD_DIM, HEAD_DIM))
    half_low = near((heads // 2, tokens // BLOCK, HEAD_DIM, HEAD_DIM), BF16)
    half_wide = near((tokens, width // 2), BF16)
    half_full = near((tokens, width // 2))
    sums_shape = near((2, tokens))
    grads = pltpu.HBM((tokens, width), BF16)
    states = [near((len(steps), HEAD_DIM, HEAD_DIM)) for steps in STEPS]
    *other, sooner_1, keys_0, keys_1, values_0, values_1 = call(
        other_totals_kernel,
        (*states, inner_blocks, *[half_wide] * 4),
        far=2,
        scratch_shapes=[pltpu.SemaphoreType.DMA((2, 2, 4))],
    )(keys, values)
    *mine, sooner_0 = call(key_value_states, (*states, inner_blocks))(keys_0, values_0)
    sooner, keys, values = (sooner_0, sooner_1), (keys_0, keys_1), (values_0, values_1)

    def beside_forward(after):
        return call(
            within_kernel,
            (full, full, wide),
            far=3,
            scratch_shapes=[wide, near((1, width), BF16), pltpu.SemaphoreType.DMA((3, 2))],
        )(queries, out_grad, gain, *keys, *values, after)

    entered, (within, upstream, queries), _ = entering(
        mine, other, False, beside_forward, lambda after: ()
    )
    outputs, lows, sums = [], [], []
    for part, state in enumerate(entered):
        output, low, *sums = call(
            functools.partial(forward_kernel, part), (half_full, half_low, sums_shape)
        )(queries, upstream, within, state, sooner[part], *sums)
        outputs.append(output)
        lows.append(low)
    sums = swaps(sums * lax.axis_size("head"), "head", (1, 3, 2)) + sums
    results = [
        call(functools.partial(delta_kernel, part), (half_wide, *states, inner_blocks))(
            queries, upstream, outputs[part], *sums
        )
        for part in (1, 0)
    ][::-1]
    deltas = [result[0] for result in results]
    later = [result[3] for result in results]

    def inner_grads(after):
        made = []
        for part in range(2):
            made += call(functools.partial(inner_kernel, part), (half_full, half_full))(
                queries, keys[part], values[part], deltas[part], after
            )
        return made

    def query_grads(after):
        return (
            call(
                query_kernel,
                grads,
                scratch_shapes=[half_wide, half_wide, pltpu.SemaphoreType.DMA((2,))],
            )(*keys, *values, *deltas, *lows, after),
        )

    entered, inner, (query_grad,) = entering(
        results[0][1:3], results[1][1:3], True, inner_grads, query_grads
    )
    key_0, value_0 = call(backward_kernel, (half_wide, half_wide))(
        keys[0], values[0], *inner[:2], entered[0], later[0]
    )
    key_grad, value_grad = call(
        last_kernel,
        (grads, grads),
        scratch_shapes=[half_wide, half_wide, pltpu.SemaphoreType.DMA((4,))],
    )(keys[1], values[1], *inner[2:], entered[1], later[1], key_0, value_0)
    return query_grad, key_grad, value_grad


def solution(mesh):
    _, across = mesh.devices.shape
    shape = (4, 2, 4, 2, across)
    inner = Mesh(mesh.devices.reshape(shape), ("row", "high", "low", "core", "head"))
    spec = P(("row", "high", "low", "core"), "head")
    return jax.shard_map(
        on_device,
        mesh=inner,
        in_specs=(spec, spec, spec, spec, P("head")),
        out_specs=(spec, spec, spec),
        check_vma=False,
    )
```

```python
import functools

import jax
import jax.numpy as jnp
from jax import lax
from jax.experimental import pallas as pl
from jax.experimental.pallas import tpu as pltpu
from jax.sharding import Mesh
from jax.sharding import PartitionSpec as P

HEADS = 32
HEAD_DIM = 128
BLOCK = 128
EPSILON = 1e-05
FEATURES = HEADS * HEAD_DIM
FACTOR = HEAD_DIM ** (-0.5)
F32 = jnp.float32
BF16 = jnp.bfloat16
VMEM_LIMIT = 16 * 1024 * 1024
COST = pl.CostEstimate(flops=10**9, bytes_accessed=2**21, transcendentals=0)
STEPS = ((3,), (2, 1, 0))
BACK = ((0, 3, 2), (1,))


def dot_nn(a, b):
    return lax.dot_general(a, b, (((1,), (0,)), ((), ())), preferred_element_type=F32)


def dot_nt(a, b):
    return lax.dot_general(a, b, (((1,), (1,)), ((), ())), preferred_element_type=F32)


def dot_tn(a, b):
    return lax.dot_general(a, b, (((0,), (0,)), ((), ())), preferred_element_type=F32)


def columns(head):
    return pl.ds(head * HEAD_DIM, HEAD_DIM)


def columns_of(part, step, heads):
    head = part * heads + (owner() ^ step)
    return pl.ds(pl.multiple_of(head * HEAD_DIM, HEAD_DIM), HEAD_DIM)


def blocks(tokens):
    return [slice(at, at + BLOCK) for at in range(0, tokens, BLOCK)]


def causal(count, transposed):
    row = lax.broadcasted_iota(jnp.int32, (count, count), 0)
    col = lax.broadcasted_iota(jnp.int32, (count, count), 1)
    order = row <= col if transposed else col <= row
    return order & (row // BLOCK == col // BLOCK)


def scores(a, b, mask):
    return jnp.where(mask, dot_nt(a, b) * FACTOR, 0.0).astype(BF16)


def here(name):
    return lax.axis_index(name)


def near(shape, dtype=F32):
    return pltpu.VMEM(shape, dtype)


def call(kernel, out_shape, far=0, loose=0, **kwargs):
    def run(*operands):
        close = len(operands) - far - loose
        spaces = [pltpu.HBM] * far + [pltpu.VMEM] * close + [pl.ANY] * loose
        return pl.pallas_call(
            kernel,
            out_shape=out_shape,
            in_specs=[pl.BlockSpec(memory_space=space) for space in spaces],
            compiler_params=pltpu.CompilerParams(vmem_limit_bytes=VMEM_LIMIT),
            cost_estimate=COST,
            **kwargs,
        )(*map(pltpu.with_memory_space_constraint, operands, spaces))

    return run


def halves(far, near, sems):
    half = far.shape[1] // 2
    result = []
    for part in range(2):
        core = 1 - here("core") if part else here("core")
        there = pl.ds(pl.multiple_of(core * half, half), half)
        result.append((far.at[:, there], near.at[:, pl.ds(part * half, half)], sems.at[part]))
    return result


def fetch(far, near, sems):
    return [pltpu.make_async_copy(there, at, sem) for there, at, sem in halves(far, near, sems)]


def key_value_states(keys, values, first, rest, sooner):
    heads = keys.shape[1] // HEAD_DIM
    for out, steps in zip((first, rest), STEPS):
        for index, step in enumerate(steps):
            at = columns_of(0, step, heads)
            total = jnp.zeros(out.shape[1:], F32)
            for block, rows in enumerate(blocks(keys.shape[0])):
                if block:
                    sooner[owner() ^ step, block - 1] = total
                total = total + dot_tn(keys[rows, at], values[rows, at])
            out[index] = total


def other_totals_kernel(
    keys_far, values_far, first, rest, sooner, keys_0, keys_1, values_0, values_1, sems
):
    chunks = sems.shape[2]
    rows = keys_0.shape[0] // chunks
    half = keys_0.shape[1]
    copies = []
    for part, arrays in ((1, (keys_1, values_1)), (0, (keys_0, values_0))):
        core = 1 - here("core") if part else here("core")
        there = pl.ds(pl.multiple_of(core * half, half), half)
        group = []
        for which, (far, near) in enumerate(zip((keys_far, values_far), arrays)):
            for chunk in range(chunks):
                at = pl.ds(chunk * rows, rows)
                copy = pltpu.make_async_copy(
                    far.at[at, there], near.at[at], sems.at[part, which, chunk]
                )
                copy.start()
                group.append(copy)
        copies.append(group)
    for copy in copies[0]:
        copy.wait()
    key_value_states(keys_1, values_1, first, rest, sooner)
    for copy in copies[1]:
        copy.wait()


def within_kernel(
    queries_far, grad_far, gain_far, keys_0, keys_1, values_0, values_1, after,
    within, upstream, queries, grad, gain, sems,
):
    del after
    copies = [
        fetch(queries_far, queries, sems.at[0]),
        fetch(grad_far, grad, sems.at[1]),
        fetch(gain_far, gain, sems.at[2]),
    ]
    for pair in copies:
        for copy in pair:
            copy.start()
    mask = causal(queries.shape[0], False)
    for pair in copies:
        for copy in pair:
            copy.wait()
    heads = queries.shape[1] // HEAD_DIM // 2
    for part, (keys, values) in enumerate(((keys_0, values_0), (keys_1, values_1))):
        for head in range(heads):
            at, near = columns(part * heads + head), columns(head)
            within[:, at] = dot_nn(scores(queries[:, at], keys[:, near], mask), values[:, near])
            upstream[:, at] = grad[:, at].astype(F32) * gain[:, at].astype(F32)


def split_kernel(mine, got, *pieces):
    for index, piece in enumerate(pieces):
        piece[...] = mine[index] + got[index]


def join_kernel(skip, count, *refs):
    parts = refs[skip : skip + count]
    total = parts[0][...]
    for part in parts[1:]:
        total = total + part[...]
    refs[-1][...] = total


def members_kernel(reverse, group, rows, *refs):
    parts, refs = refs[:group], refs[group:]
    mirror, there, outs = refs[0], refs[1:rows], refs[rows:]
    row, low, high = here("row"), here("low"), here("high")
    ahead = jnp.where(before(1 - high, high, reverse), mirror[...], 0.0)
    for step in range(1, rows):
        sooner = before(row ^ step, row, reverse)
        ahead = ahead + jnp.where(sooner, there[step - 1][...], 0.0)
    for at, out in enumerate(outs):
        result = ahead
        for step in range(group):
            if step != at:
                sooner = before(low ^ step, low ^ at, reverse)
                result = result + jnp.where(sooner, parts[step][...], 0.0)
        out[...] = result


def merge_kernel(reverse, steps, *refs):
    back, refs = refs[: len(steps)], refs[len(steps) :]
    mine, got, (own, theirs) = refs[:2], refs[2:4], refs[4:]
    first = before(here("core"), 1 - here("core"), reverse)
    for index, step in enumerate(steps):
        which = int(step not in STEPS[0])
        at = STEPS[which].index(step)
        own[index] = back[index][...] + jnp.where(first, 0.0, got[which][at])
        theirs[index] = back[index][...] + jnp.where(first, mine[which][at], 0.0)


def forward_kernel(part, steps, last, queries, upstream, within, state, sooner, *refs):
    outputs = 3 if last else 4
    earlier, (output, low, *sums) = refs[:-outputs], refs[-outputs:]
    heads = sooner.shape[0]
    tokens = queries.shape[0]
    if earlier:
        square, mixed = (ref[...] for ref in earlier)
    else:
        square = mixed = jnp.zeros((tokens, HEAD_DIM), F32)
    for index, step in enumerate(steps):
        at = columns_of(part, step, heads)
        carried = []
        for block, rows in enumerate(blocks(tokens)):
            wide = state[index]
            if block:
                wide = wide + sooner[owner() ^ step, block - 1]
            state_low = wide.astype(BF16)
            low[index, block] = state_low
            carried.append(dot_nn(queries[rows, at], state_low))
        out = within[:, at] + FACTOR * jnp.concatenate(carried)
        output[:, columns(index)] = out
        square = square + out * out
        mixed = mixed + upstream[:, at] * out
    for row, array in enumerate((square, mixed)):
        if last:
            sums[0][row : row + 1] = jnp.sum(array.T, axis=0, keepdims=True)
        else:
            sums[row][...] = array


def delta_kernel(part, queries, upstream, output_a, output_b, *refs):
    sums, (delta, first, rest, later) = refs[:4], refs[4:]
    tokens = queries.shape[0]
    heads = delta.shape[1] // HEAD_DIM
    total = sums[0][...] + sums[1][...] + sums[2][...] + sums[3][...]
    inv_rms = lax.rsqrt(total[0:1] / FEATURES + EPSILON)
    pull = inv_rms * inv_rms * inv_rms * (total[1:2] / FEATURES)
    inv_rms = jnp.broadcast_to(inv_rms, (HEAD_DIM, tokens)).T
    pull = jnp.broadcast_to(pull, (HEAD_DIM, tokens)).T
    for back, steps in zip((first, rest), STEPS):
        for index, step in enumerate(steps):
            which = int(step not in BACK[0])
            output = (output_a, output_b)[which][:, columns(BACK[which].index(step))]
            at = columns_of(part, step, heads)
            out_delta = (inv_rms * upstream[:, at] - pull * output).astype(BF16)
            delta[:, columns_of(0, step, heads)] = out_delta
            total = jnp.zeros(back.shape[1:], F32)
            parts = blocks(tokens)
            for block in reversed(range(len(parts))):
                rows = parts[block]
                if block + 1 < len(parts):
                    later[owner() ^ step, block] = total
                total = total + dot_tn(out_delta[rows], queries[rows, at])
            back[index] = total


def write(near, far, part, sem):
    half = near.shape[1]
    core = 1 - here("core") if part else here("core")
    there = pl.ds(pl.multiple_of(core * half, half), half)
    copy = pltpu.make_async_copy(near, far.at[:, there], sem)
    copy.start()
    return copy


def query_kernel(*refs):
    *operands, _, far, near_0, near_1, sems = refs
    mask = causal(operands[0].shape[0], False)
    copies = []
    for part, near in enumerate((near_0, near_1)):
        keys, values, delta, *lows = operands[part::2]
        heads = near.shape[1] // HEAD_DIM
        for low, steps in zip(lows, BACK):
            for index, step in enumerate(steps):
                at = columns_of(0, step, heads)
                out_delta = delta[:, at]
                carried = [
                    dot_nt(out_delta[rows], low[index, block])
                    for block, rows in enumerate(blocks(keys.shape[0]))
                ]
                delta_scores = scores(out_delta, values[:, at], mask)
                grad = dot_nn(delta_scores, keys[:, at]) + FACTOR * jnp.concatenate(carried)
                near[:, at] = grad.astype(BF16)
        copies.append(write(near, far, part, sems.at[part]))
    for copy in copies:
        copy.wait()


def inner_kernel(part, queries, keys, values, delta, after, key_inner, value_inner):
    del after
    mask = causal(keys.shape[0], True)
    heads = delta.shape[1] // HEAD_DIM
    for head in range(heads):
        at = columns(head)
        query, out_delta = queries[:, columns(part * heads + head)], delta[:, at]
        key_inner[:, at] = dot_nn(scores(values[:, at], out_delta, mask), query)
        value_inner[:, at] = dot_nn(scores(keys[:, at], query, mask), out_delta)


def backward_kernel(
    steps, keys, values, key_inner, value_inner, state, later, key_near, value_near
):
    parts = blocks(keys.shape[0])
    heads = later.shape[0]
    for index, step in enumerate(steps):
        at = columns_of(0, step, heads)
        lows = []
        for block in range(len(parts)):
            wide = state[index]
            if block + 1 < len(parts):
                wide = wide + later[owner() ^ step, block]
            lows.append(wide.astype(BF16))
        carried = [dot_nn(values[rows, at], lows[n]) for n, rows in enumerate(parts)]
        grad = key_inner[:, at] + FACTOR * jnp.concatenate(carried)
        key_near[:, columns(index)] = grad.astype(BF16)
        carried = [dot_nt(keys[rows, at], lows[n]) for n, rows in enumerate(parts)]
        grad = value_inner[:, at] + FACTOR * jnp.concatenate(carried)
        value_near[:, columns(index)] = grad.astype(BF16)


def last_kernel(*refs):
    operands, ready, refs = refs[:6], refs[6:12], refs[12:]
    (key_far, value_far), (key_last, value_last, sems) = refs[:2], refs[2:]
    heads = operands[5].shape[0]
    copies = []

    def send(part, steps, pair):
        core = 1 - here("core") if part else here("core")
        for near, far in zip(pair, (key_far, value_far)):
            for index, step in enumerate(steps):
                there = columns_of(core, step, heads)
                copy = pltpu.make_async_copy(
                    near.at[:, columns(index)], far.at[:, there], sems.at[len(copies)]
                )
                copy.start()
                copies.append(copy)

    for turn, (part, steps) in enumerate(((0, BACK[0]), (0, BACK[1]), (1, BACK[0]))):
        send(part, steps, ready[2 * turn : 2 * turn + 2])
    backward_kernel(BACK[1], *operands, key_last, value_last)
    send(1, BACK[1], (key_last, value_last))
    for copy in copies:
        copy.wait()


def swap(array, axis, distance):
    count = lax.axis_size(axis)
    return lax.ppermute(array, axis, [(at, at ^ distance) for at in range(count)])


def before(one, other, reverse):
    return one > other if reverse else one < other


def owner():
    return here("low") ^ (lax.axis_size("low") // 2 * here("high"))


def swaps(arrays, axis, order):
    there = {step: swap(arrays[step], axis, step) for step in order}
    return [there[step] for step in sorted(there)]


def entering(mine, other, reverse, beside):
    group, rows = lax.axis_size("low"), lax.axis_size("row")
    line, ring = (3, 2, 1), (1, 3, 2)
    piece = near(mine[0].shape[1:])
    got = [swap(array, "core", 1) for array in other]
    parts = {}
    for steps, *arrays in zip(STEPS, mine, got):
        parts.update(zip(steps, call(split_kernel, [piece] * len(steps))(*arrays)))
    made = beside(parts[0])
    parts = [parts[0]] + swaps(parts, "low", line)
    first, *ties = made
    whole = call(functools.partial(join_kernel, int(reverse), group), piece, far=int(reverse))(
        *((first, *parts) if reverse else (*parts, first)), *ties
    )
    mirror = swap(whole, ("high", "low"), group + group // 2)
    whole = call(functools.partial(join_kernel, 0, 2), piece)(whole, mirror)
    there = swaps([whole] * rows, "row", ring)
    back = call(functools.partial(members_kernel, reverse, group, rows), [piece] * group)(
        *parts, mirror, *there
    )
    back = [back[0]] + swaps(back, "low", line)
    states = []
    for steps in BACK:
        shape = near((len(steps), *mine[0].shape[1:]))
        own, theirs = call(functools.partial(merge_kernel, reverse, steps), (shape, shape))(
            *(back[step] for step in steps), *mine, *got
        )
        states.append((own, swap(theirs, "core", 1)))
    return list(zip(*states)), made


def on_device(queries, keys, values, out_grad, gain):
    tokens, width = queries.shape
    heads = width // HEAD_DIM
    gain = gain.reshape(1, width)
    wide = near((tokens, width), BF16)
    full = near((tokens, width))
    count = heads // 2
    states = [near((len(steps), HEAD_DIM, HEAD_DIM)) for steps in STEPS]
    inner_blocks = near((count, tokens // BLOCK - 1, HEAD_DIM, HEAD_DIM))
    half_wide = near((tokens, width // 2), BF16)
    half_full = near((tokens, width // 2))
    lane_full = near((tokens, HEAD_DIM))
    grads = pltpu.HBM((tokens, width), BF16)
    *other, sooner_1, keys_0, keys_1, values_0, values_1 = call(
        other_totals_kernel,
        (*states, inner_blocks, *[half_wide] * 4),
        far=2,
        scratch_shapes=[pltpu.SemaphoreType.DMA((2, 2, 4))],
    )(keys, values)
    *mine, sooner_0 = call(key_value_states, (*states, inner_blocks))(keys_0, values_0)
    sooner, keys, values = (sooner_0, sooner_1), (keys_0, keys_1), (values_0, values_1)

    def beside_forward(after):
        return call(
            within_kernel,
            (full, full, wide),
            far=3,
            scratch_shapes=[wide, near((1, width), BF16), pltpu.SemaphoreType.DMA((3, 2))],
        )(queries, out_grad, gain, *keys, *values, after)

    entered, (within, upstream, queries) = entering(mine, other, False, beside_forward)
    outputs, lows, sums = [], [], []
    for part in range(2):
        for turn, steps in enumerate(BACK):
            last = bool(part and turn)
            output, low, *sums = call(
                functools.partial(forward_kernel, part, steps, last),
                (
                    near((tokens, len(steps) * HEAD_DIM)),
                    near((len(steps), tokens // BLOCK, HEAD_DIM, HEAD_DIM), BF16),
                    *([near((2, tokens))] if last else [lane_full] * 2),
                ),
            )(queries, upstream, within, entered[part][turn], sooner[part], *sums)
            outputs.append(output)
            lows.append(low)
    sums = swaps(sums * lax.axis_size("head"), "head", (1, 3, 2)) + sums
    results = [
        call(
            functools.partial(delta_kernel, part), (half_wide, *states, inner_blocks)
        )(queries, upstream, *outputs[2 * part : 2 * part + 2], *sums)
        for part in (1, 0)
    ][::-1]
    deltas = [result[0] for result in results]
    later = [result[3] for result in results]

    def beside_backward(after):
        query_grad = call(
            query_kernel,
            grads,
            scratch_shapes=[half_wide, half_wide, pltpu.SemaphoreType.DMA((2,))],
        )(*keys, *values, *deltas, *lows[::2], *lows[1::2], after)
        inner = [
            call(functools.partial(inner_kernel, part), (half_full, half_full))(
                queries, keys[part], values[part], deltas[part], after
            )
            for part in range(2)
        ]
        return query_grad, *inner[0], *inner[1]

    entered, (query_grad, *inner) = entering(
        results[0][1:3], results[1][1:3], True, beside_backward
    )
    ready = []
    for part in range(2):
        for turn, steps in enumerate(BACK):
            operands = (
                keys[part], values[part], *inner[2 * part : 2 * part + 2],
                entered[part][turn], later[part],
            )
            shape = near((tokens, len(steps) * HEAD_DIM), BF16)
            if not (part and turn):
                ready += call(functools.partial(backward_kernel, steps), (shape, shape))(
                    *operands
                )
    key_grad, value_grad = call(
        last_kernel,
        (grads, grads),
        scratch_shapes=[shape, shape, pltpu.SemaphoreType.DMA((2 * heads,))],
    )(*operands, *ready)
    return query_grad, key_grad, value_grad


def solution(mesh):
    _, across = mesh.devices.shape
    shape = (4, 2, 4, 2, across)
    inner = Mesh(mesh.devices.reshape(shape), ("row", "high", "low", "core", "head"))
    spec = P(("row", "high", "low", "core"), "head")
    return jax.shard_map(
        on_device,
        mesh=inner,
        in_specs=(spec, spec, spec, spec, P("head")),
        out_specs=(spec, spec, spec),
        check_vma=False,
    )
```

```python
import functools

import jax
import jax.numpy as jnp
from jax import lax
from jax.experimental import pallas as pl
from jax.experimental.pallas import tpu as pltpu
from jax.sharding import Mesh
from jax.sharding import PartitionSpec as P

HEADS = 32
HEAD_DIM = 128
BLOCK = 128
EPSILON = 1e-05
FEATURES = HEADS * HEAD_DIM
FACTOR = HEAD_DIM ** (-0.5)
F32 = jnp.float32
BF16 = jnp.bfloat16
VMEM_LIMIT = 16 * 1024 * 1024
COST = pl.CostEstimate(flops=10**9, bytes_accessed=2**21, transcendentals=0)
STEPS = ((3,), (2, 1, 0))
BACK = ((0, 3, 2), (1,))


def dot_nn(a, b):
    return lax.dot_general(a, b, (((1,), (0,)), ((), ())), preferred_element_type=F32)


def dot_nt(a, b):
    return lax.dot_general(a, b, (((1,), (1,)), ((), ())), preferred_element_type=F32)


def dot_tn(a, b):
    return lax.dot_general(a, b, (((0,), (0,)), ((), ())), preferred_element_type=F32)


def columns(head):
    return pl.ds(head * HEAD_DIM, HEAD_DIM)


def columns_of(part, step, heads):
    head = part * heads + (owner() ^ step)
    return pl.ds(pl.multiple_of(head * HEAD_DIM, HEAD_DIM), HEAD_DIM)


def blocks(tokens):
    return [slice(at, at + BLOCK) for at in range(0, tokens, BLOCK)]


def causal(count, transposed):
    row = lax.broadcasted_iota(jnp.int32, (count, count), 0)
    col = lax.broadcasted_iota(jnp.int32, (count, count), 1)
    order = row <= col if transposed else col <= row
    return order & (row // BLOCK == col // BLOCK)


def scores(a, b, mask):
    return jnp.where(mask, dot_nt(a, b) * FACTOR, 0.0).astype(BF16)


def here(name):
    return lax.axis_index(name)


def near(shape, dtype=F32):
    return pltpu.VMEM(shape, dtype)


def call(kernel, out_shape, far=0, loose=0, **kwargs):
    def run(*operands):
        close = len(operands) - far - loose
        spaces = [pltpu.HBM] * far + [pltpu.VMEM] * close + [pl.ANY] * loose
        return pl.pallas_call(
            kernel,
            out_shape=out_shape,
            in_specs=[pl.BlockSpec(memory_space=space) for space in spaces],
            compiler_params=pltpu.CompilerParams(vmem_limit_bytes=VMEM_LIMIT),
            cost_estimate=COST,
            **kwargs,
        )(*map(pltpu.with_memory_space_constraint, operands, spaces))

    return run


def halves(far, near, sems):
    half = far.shape[1] // 2
    result = []
    for part in range(2):
        core = 1 - here("core") if part else here("core")
        there = pl.ds(pl.multiple_of(core * half, half), half)
        result.append((far.at[:, there], near.at[:, pl.ds(part * half, half)], sems.at[part]))
    return result


def fetch(far, near, sems):
    return [pltpu.make_async_copy(there, at, sem) for there, at, sem in halves(far, near, sems)]


def key_value_states(keys, values, first, rest, sooner):
    heads = keys.shape[1] // HEAD_DIM
    for out, steps in zip((first, rest), STEPS):
        for index, step in enumerate(steps):
            at = columns_of(0, step, heads)
            total = jnp.zeros(out.shape[1:], F32)
            for block, rows in enumerate(blocks(keys.shape[0])):
                if block:
                    sooner[owner() ^ step, block - 1] = total
                total = total + dot_tn(keys[rows, at], values[rows, at])
            out[index] = total


def other_totals_kernel(
    keys_far, values_far, first, rest, sooner, keys_0, keys_1, values_0, values_1, sems
):
    chunks = sems.shape[2]
    rows = keys_0.shape[0] // chunks
    half = keys_0.shape[1]
    copies = []
    for part, arrays in ((1, (keys_1, values_1)), (0, (keys_0, values_0))):
        core = 1 - here("core") if part else here("core")
        there = pl.ds(pl.multiple_of(core * half, half), half)
        group = []
        for which, (far, near) in enumerate(zip((keys_far, values_far), arrays)):
            for chunk in range(chunks):
                at = pl.ds(chunk * rows, rows)
                copy = pltpu.make_async_copy(
                    far.at[at, there], near.at[at], sems.at[part, which, chunk]
                )
                copy.start()
                group.append(copy)
        copies.append(group)
    for copy in copies[0]:
        copy.wait()
    key_value_states(keys_1, values_1, first, rest, sooner)
    for copy in copies[1]:
        copy.wait()


def within_kernel(
    queries_far, grad_far, gain_far, keys_0, keys_1, values_0, values_1, after,
    within, upstream, queries, grad, gain, sems,
):
    del after
    copies = [
        fetch(queries_far, queries, sems.at[0]),
        fetch(grad_far, grad, sems.at[1]),
        fetch(gain_far, gain, sems.at[2]),
    ]
    for pair in copies:
        for copy in pair:
            copy.start()
    mask = causal(queries.shape[0], False)
    for pair in copies:
        for copy in pair:
            copy.wait()
    heads = queries.shape[1] // HEAD_DIM // 2
    for part, (keys, values) in enumerate(((keys_0, values_0), (keys_1, values_1))):
        for head in range(heads):
            at, near = columns(part * heads + head), columns(head)
            within[:, at] = dot_nn(scores(queries[:, at], keys[:, near], mask), values[:, near])
            upstream[:, at] = grad[:, at].astype(F32) * gain[:, at].astype(F32)


def split_kernel(mine, got, *pieces):
    for index, piece in enumerate(pieces):
        piece[...] = mine[index] + got[index]


def join_kernel(skip, count, *refs):
    parts = refs[skip : skip + count]
    total = parts[0][...]
    for part in parts[1:]:
        total = total + part[...]
    refs[-1][...] = total


def members_kernel(reverse, group, rows, *refs):
    parts, refs = refs[:group], refs[group:]
    mirror, there, outs = refs[0], refs[1:rows], refs[rows:]
    row, low, high = here("row"), here("low"), here("high")
    ahead = jnp.where(before(1 - high, high, reverse), mirror[...], 0.0)
    for step in range(1, rows):
        sooner = before(row ^ step, row, reverse)
        ahead = ahead + jnp.where(sooner, there[step - 1][...], 0.0)
    for at, out in enumerate(outs):
        result = ahead
        for step in range(group):
            if step != at:
                sooner = before(low ^ step, low ^ at, reverse)
                result = result + jnp.where(sooner, parts[step][...], 0.0)
        out[...] = result


def merge_kernel(reverse, steps, *refs):
    back, refs = refs[: len(steps)], refs[len(steps) :]
    mine, got, (own, theirs) = refs[:2], refs[2:4], refs[4:]
    first = before(here("core"), 1 - here("core"), reverse)
    for index, step in enumerate(steps):
        which = int(step not in STEPS[0])
        at = STEPS[which].index(step)
        own[index] = back[index][...] + jnp.where(first, 0.0, got[which][at])
        theirs[index] = back[index][...] + jnp.where(first, mine[which][at], 0.0)


def forward_kernel(part, steps, last, queries, upstream, within, state, sooner, *refs):
    outputs = 3 if last else 4
    earlier, (output, low, *sums) = refs[:-outputs], refs[-outputs:]
    heads = sooner.shape[0]
    tokens = queries.shape[0]
    if earlier:
        square, mixed = (ref[...] for ref in earlier)
    else:
        square = mixed = jnp.zeros((tokens, HEAD_DIM), F32)
    for index, step in enumerate(steps):
        at = columns_of(part, step, heads)
        carried = []
        for block, rows in enumerate(blocks(tokens)):
            wide = state[index]
            if block:
                wide = wide + sooner[owner() ^ step, block - 1]
            state_low = wide.astype(BF16)
            low[index, block] = state_low
            carried.append(dot_nn(queries[rows, at], state_low))
        out = within[:, at] + FACTOR * jnp.concatenate(carried)
        output[:, columns(index)] = out
        square = square + out * out
        mixed = mixed + upstream[:, at] * out
    for row, array in enumerate((square, mixed)):
        if last:
            sums[0][row : row + 1] = jnp.sum(array.T, axis=0, keepdims=True)
        else:
            sums[row][...] = array


def delta_kernel(part, queries, upstream, output_a, output_b, *refs):
    sums, (delta, first, rest, later) = refs[:4], refs[4:]
    tokens = queries.shape[0]
    heads = delta.shape[1] // HEAD_DIM
    total = sums[0][...] + sums[1][...] + sums[2][...] + sums[3][...]
    inv_rms = lax.rsqrt(total[0:1] / FEATURES + EPSILON)
    pull = inv_rms * inv_rms * inv_rms * (total[1:2] / FEATURES)
    inv_rms = jnp.broadcast_to(inv_rms, (HEAD_DIM, tokens)).T
    pull = jnp.broadcast_to(pull, (HEAD_DIM, tokens)).T
    for back, steps in zip((first, rest), STEPS):
        for index, step in enumerate(steps):
            which = int(step not in BACK[0])
            output = (output_a, output_b)[which][:, columns(BACK[which].index(step))]
            at = columns_of(part, step, heads)
            out_delta = (inv_rms * upstream[:, at] - pull * output).astype(BF16)
            delta[:, columns_of(0, step, heads)] = out_delta
            total = jnp.zeros(back.shape[1:], F32)
            parts = blocks(tokens)
            for block in reversed(range(len(parts))):
                rows = parts[block]
                if block + 1 < len(parts):
                    later[owner() ^ step, block] = total
                total = total + dot_tn(out_delta[rows], queries[rows, at])
            back[index] = total


def write(near, far, part, sem):
    half = near.shape[1]
    core = 1 - here("core") if part else here("core")
    there = pl.ds(pl.multiple_of(core * half, half), half)
    copy = pltpu.make_async_copy(near, far.at[:, there], sem)
    copy.start()
    return copy


def query_kernel(*refs):
    *operands, _, far, near_0, near_1, sems = refs
    mask = causal(operands[0].shape[0], False)
    copies = []
    for part, near in enumerate((near_0, near_1)):
        keys, values, delta, *lows = operands[part::2]
        heads = near.shape[1] // HEAD_DIM
        for low, steps in zip(lows, BACK):
            for index, step in enumerate(steps):
                at = columns_of(0, step, heads)
                out_delta = delta[:, at]
                carried = [
                    dot_nt(out_delta[rows], low[index, block])
                    for block, rows in enumerate(blocks(keys.shape[0]))
                ]
                delta_scores = scores(out_delta, values[:, at], mask)
                grad = dot_nn(delta_scores, keys[:, at]) + FACTOR * jnp.concatenate(carried)
                near[:, at] = grad.astype(BF16)
        copies.append(write(near, far, part, sems.at[part]))
    for copy in copies:
        copy.wait()


def inner_kernel(part, queries, keys, values, delta, after, key_inner, value_inner):
    del after
    mask = causal(keys.shape[0], True)
    heads = delta.shape[1] // HEAD_DIM
    for head in range(heads):
        at = columns(head)
        query, out_delta = queries[:, columns(part * heads + head)], delta[:, at]
        key_inner[:, at] = dot_nn(scores(values[:, at], out_delta, mask), query)
        value_inner[:, at] = dot_nn(scores(keys[:, at], query, mask), out_delta)


def head_grads(step, operands, state, key_near, value_near, near_at):
    keys, values, key_inner, value_inner, later = operands
    parts = blocks(keys.shape[0])
    at = columns_of(0, step, later.shape[0])
    lows = []
    for block in range(len(parts)):
        wide = state
        if block + 1 < len(parts):
            wide = wide + later[owner() ^ step, block]
        lows.append(wide.astype(BF16))
    carried = [dot_nn(values[rows, at], lows[n]) for n, rows in enumerate(parts)]
    grad = key_inner[:, at] + FACTOR * jnp.concatenate(carried)
    key_near[:, near_at] = grad.astype(BF16)
    carried = [dot_nt(keys[rows, at], lows[n]) for n, rows in enumerate(parts)]
    grad = value_inner[:, at] + FACTOR * jnp.concatenate(carried)
    value_near[:, near_at] = grad.astype(BF16)


def own_kernel(*refs):
    operands, states, nears = refs[:5], refs[5:7], refs[7:]
    for state, steps in zip(states, BACK):
        for index, step in enumerate(steps):
            at = columns_of(0, step, operands[4].shape[0])
            head_grads(step, operands, state[index], *nears, at)


def backward_kernel(steps, *refs):
    operands, state, nears = refs[:5], refs[5], refs[6:]
    for index, step in enumerate(steps):
        head_grads(step, operands, state[index], *nears, columns(index))


def last_kernel(*refs):
    operands, (key_0, value_0, key_1, value_1), refs = refs[:6], refs[6:10], refs[10:]
    (key_far, value_far), (key_last, value_last, sems) = refs[:2], refs[2:]
    heads = operands[4].shape[0]
    copies = [
        write(key_0, key_far, 0, sems.at[0]),
        write(value_0, value_far, 0, sems.at[1]),
    ]

    def send(steps, pair):
        for near, far in zip(pair, (key_far, value_far)):
            for index, step in enumerate(steps):
                there = columns_of(1 - here("core"), step, heads)
                copy = pltpu.make_async_copy(
                    near.at[:, columns(index)], far.at[:, there], sems.at[len(copies)]
                )
                copy.start()
                copies.append(copy)

    send(BACK[0], (key_1, value_1))
    backward_kernel(BACK[1], *operands, key_last, value_last)
    send(BACK[1], (key_last, value_last))
    for copy in copies:
        copy.wait()


def swap(array, axis, distance):
    count = lax.axis_size(axis)
    return lax.ppermute(array, axis, [(at, at ^ distance) for at in range(count)])


def before(one, other, reverse):
    return one > other if reverse else one < other


def owner():
    return here("low") ^ (lax.axis_size("low") // 2 * here("high"))


def swaps(arrays, axis, order):
    there = {step: swap(arrays[step], axis, step) for step in order}
    return [there[step] for step in sorted(there)]


def entering(mine, other, reverse, beside):
    group, rows = lax.axis_size("low"), lax.axis_size("row")
    line, ring = (3, 2, 1), (1, 3, 2)
    piece = near(mine[0].shape[1:])
    got = [swap(array, "core", 1) for array in other]
    parts = {}
    for steps, *arrays in zip(STEPS, mine, got):
        parts.update(zip(steps, call(split_kernel, [piece] * len(steps))(*arrays)))
    made = beside(parts[0])
    parts = [parts[0]] + swaps(parts, "low", line)
    first, *ties = made
    whole = call(functools.partial(join_kernel, int(reverse), group), piece, far=int(reverse))(
        *((first, *parts) if reverse else (*parts, first)), *ties
    )
    mirror = swap(whole, ("high", "low"), group + group // 2)
    whole = call(functools.partial(join_kernel, 0, 2), piece)(whole, mirror)
    there = swaps([whole] * rows, "row", ring)
    back = call(functools.partial(members_kernel, reverse, group, rows), [piece] * group)(
        *parts, mirror, *there
    )
    back = [back[0]] + swaps(back, "low", line)
    states = []
    for steps in BACK:
        shape = near((len(steps), *mine[0].shape[1:]))
        own, theirs = call(functools.partial(merge_kernel, reverse, steps), (shape, shape))(
            *(back[step] for step in steps), *mine, *got
        )
        states.append((own, swap(theirs, "core", 1)))
    return list(zip(*states)), made


def on_device(queries, keys, values, out_grad, gain):
    tokens, width = queries.shape
    heads = width // HEAD_DIM
    gain = gain.reshape(1, width)
    wide = near((tokens, width), BF16)
    full = near((tokens, width))
    count = heads // 2
    states = [near((len(steps), HEAD_DIM, HEAD_DIM)) for steps in STEPS]
    inner_blocks = near((count, tokens // BLOCK - 1, HEAD_DIM, HEAD_DIM))
    half_wide = near((tokens, width // 2), BF16)
    half_full = near((tokens, width // 2))
    lane_full = near((tokens, HEAD_DIM))
    grads = pltpu.HBM((tokens, width), BF16)
    *other, sooner_1, keys_0, keys_1, values_0, values_1 = call(
        other_totals_kernel,
        (*states, inner_blocks, *[half_wide] * 4),
        far=2,
        scratch_shapes=[pltpu.SemaphoreType.DMA((2, 2, 4))],
    )(keys, values)
    *mine, sooner_0 = call(key_value_states, (*states, inner_blocks))(keys_0, values_0)
    sooner, keys, values = (sooner_0, sooner_1), (keys_0, keys_1), (values_0, values_1)

    def beside_forward(after):
        return call(
            within_kernel,
            (full, full, wide),
            far=3,
            scratch_shapes=[wide, near((1, width), BF16), pltpu.SemaphoreType.DMA((3, 2))],
        )(queries, out_grad, gain, *keys, *values, after)

    entered, (within, upstream, queries) = entering(mine, other, False, beside_forward)
    outputs, lows, sums = [], [], []
    for part in range(2):
        for turn, steps in enumerate(BACK):
            last = bool(part and turn)
            output, low, *sums = call(
                functools.partial(forward_kernel, part, steps, last),
                (
                    near((tokens, len(steps) * HEAD_DIM)),
                    near((len(steps), tokens // BLOCK, HEAD_DIM, HEAD_DIM), BF16),
                    *([near((2, tokens))] if last else [lane_full] * 2),
                ),
            )(queries, upstream, within, entered[part][turn], sooner[part], *sums)
            outputs.append(output)
            lows.append(low)
    sums = swaps(sums * lax.axis_size("head"), "head", (1, 3, 2)) + sums
    results = [
        call(
            functools.partial(delta_kernel, part), (half_wide, *states, inner_blocks)
        )(queries, upstream, *outputs[2 * part : 2 * part + 2], *sums)
        for part in (1, 0)
    ][::-1]
    deltas = [result[0] for result in results]
    later = [result[3] for result in results]

    def beside_backward(after):
        query_grad = call(
            query_kernel,
            grads,
            scratch_shapes=[half_wide, half_wide, pltpu.SemaphoreType.DMA((2,))],
        )(*keys, *values, *deltas, *lows[::2], *lows[1::2], after)
        inner = [
            call(functools.partial(inner_kernel, part), (half_full, half_full))(
                queries, keys[part], values[part], deltas[part], after
            )
            for part in range(2)
        ]
        return query_grad, *inner[0], *inner[1]

    entered, (query_grad, *inner) = entering(
        results[0][1:3], results[1][1:3], True, beside_backward
    )
    own, theirs = (
        (keys[part], values[part], *inner[2 * part : 2 * part + 2], later[part])
        for part in range(2)
    )
    ready = list(call(own_kernel, (half_wide, half_wide))(*own, *entered[0]))
    shapes = [near((tokens, len(steps) * HEAD_DIM), BF16) for steps in BACK]
    ready += call(functools.partial(backward_kernel, BACK[0]), (shapes[0], shapes[0]))(
        *theirs, entered[1][0]
    )
    key_grad, value_grad = call(
        last_kernel,
        (grads, grads),
        scratch_shapes=[shapes[1], shapes[1], pltpu.SemaphoreType.DMA((2 + heads,))],
    )(*theirs, entered[1][1], *ready)
    return query_grad, key_grad, value_grad


def solution(mesh):
    _, across = mesh.devices.shape
    shape = (4, 2, 4, 2, across)
    inner = Mesh(mesh.devices.reshape(shape), ("row", "high", "low", "core", "head"))
    spec = P(("row", "high", "low", "core"), "head")
    return jax.shard_map(
        on_device,
        mesh=inner,
        in_specs=(spec, spec, spec, spec, P("head")),
        out_specs=(spec, spec, spec),
        check_vma=False,
    )
```

```python
import functools

import jax
import jax.numpy as jnp
from jax import lax
from jax.experimental import pallas as pl
from jax.experimental.pallas import tpu as pltpu
from jax.sharding import Mesh
from jax.sharding import PartitionSpec as P

HEADS = 32
HEAD_DIM = 128
BLOCK = 128
EPSILON = 1e-05
FEATURES = HEADS * HEAD_DIM
FACTOR = HEAD_DIM ** (-0.5)
F32 = jnp.float32
BF16 = jnp.bfloat16
VMEM_LIMIT = 16 * 1024 * 1024
COST = pl.CostEstimate(flops=10**9, bytes_accessed=2**21, transcendentals=0)
STEPS = ((3,), (2, 1, 0))
BACK = ((0, 3, 2), (1,))


def dot_nn(a, b):
    return lax.dot_general(a, b, (((1,), (0,)), ((), ())), preferred_element_type=F32)


def dot_nt(a, b):
    return lax.dot_general(a, b, (((1,), (1,)), ((), ())), preferred_element_type=F32)


def dot_tn(a, b):
    return lax.dot_general(a, b, (((0,), (0,)), ((), ())), preferred_element_type=F32)


def columns(head):
    return pl.ds(head * HEAD_DIM, HEAD_DIM)


def columns_of(part, step, heads):
    head = part * heads + (owner() ^ step)
    return pl.ds(pl.multiple_of(head * HEAD_DIM, HEAD_DIM), HEAD_DIM)


def blocks(tokens):
    return [slice(at, at + BLOCK) for at in range(0, tokens, BLOCK)]


def causal(count, transposed):
    row = lax.broadcasted_iota(jnp.int32, (count, count), 0)
    col = lax.broadcasted_iota(jnp.int32, (count, count), 1)
    order = row <= col if transposed else col <= row
    return order & (row // BLOCK == col // BLOCK)


def scores(a, b, mask):
    return jnp.where(mask, dot_nt(a, b) * FACTOR, 0.0).astype(BF16)


def here(name):
    return lax.axis_index(name)


def near(shape, dtype=F32):
    return pltpu.VMEM(shape, dtype)


def call(kernel, out_shape, far=0, loose=0, **kwargs):
    def run(*operands):
        close = len(operands) - far - loose
        spaces = [pltpu.HBM] * far + [pltpu.VMEM] * close + [pl.ANY] * loose
        return pl.pallas_call(
            kernel,
            out_shape=out_shape,
            in_specs=[pl.BlockSpec(memory_space=space) for space in spaces],
            compiler_params=pltpu.CompilerParams(vmem_limit_bytes=VMEM_LIMIT),
            cost_estimate=COST,
            **kwargs,
        )(*map(pltpu.with_memory_space_constraint, operands, spaces))

    return run


def halves(far, near, sems):
    half = far.shape[1] // 2
    result = []
    for part in range(2):
        core = 1 - here("core") if part else here("core")
        there = pl.ds(pl.multiple_of(core * half, half), half)
        result.append((far.at[:, there], near.at[:, pl.ds(part * half, half)], sems.at[part]))
    return result


def fetch(far, near, sems):
    return [pltpu.make_async_copy(there, at, sem) for there, at, sem in halves(far, near, sems)]


def key_value_states(keys, values, first, rest, sooner):
    heads = keys.shape[1] // HEAD_DIM
    for out, steps in zip((first, rest), STEPS):
        for index, step in enumerate(steps):
            at = columns_of(0, step, heads)
            total = jnp.zeros(out.shape[1:], F32)
            for block, rows in enumerate(blocks(keys.shape[0])):
                if block:
                    sooner[owner() ^ step, block - 1] = total
                total = total + dot_tn(keys[rows, at], values[rows, at])
            out[index] = total


def other_totals_kernel(
    keys_far, values_far, first, rest, sooner, keys_0, keys_1, values_0, values_1, sems
):
    chunks = sems.shape[2]
    rows = keys_0.shape[0] // chunks
    half = keys_0.shape[1]
    copies = []
    for part, arrays in ((1, (keys_1, values_1)), (0, (keys_0, values_0))):
        core = 1 - here("core") if part else here("core")
        there = pl.ds(pl.multiple_of(core * half, half), half)
        group = []
        for which, (far, near) in enumerate(zip((keys_far, values_far), arrays)):
            for chunk in range(chunks):
                at = pl.ds(chunk * rows, rows)
                copy = pltpu.make_async_copy(
                    far.at[at, there], near.at[at], sems.at[part, which, chunk]
                )
                copy.start()
                group.append(copy)
        copies.append(group)
    for copy in copies[0]:
        copy.wait()
    key_value_states(keys_1, values_1, first, rest, sooner)
    for copy in copies[1]:
        copy.wait()


def within_kernel(
    queries_far, grad_far, gain_far, keys_0, keys_1, values_0, values_1, after,
    within, upstream, queries, grad, gain, sems,
):
    del after
    copies = [
        fetch(queries_far, queries, sems.at[0]),
        fetch(grad_far, grad, sems.at[1]),
        fetch(gain_far, gain, sems.at[2]),
    ]
    for pair in copies:
        for copy in pair:
            copy.start()
    mask = causal(queries.shape[0], False)
    for pair in copies:
        for copy in pair:
            copy.wait()
    heads = queries.shape[1] // HEAD_DIM // 2
    for part, (keys, values) in enumerate(((keys_0, values_0), (keys_1, values_1))):
        for head in range(heads):
            at, near = columns(part * heads + head), columns(head)
            within[:, at] = dot_nn(scores(queries[:, at], keys[:, near], mask), values[:, near])
            upstream[:, at] = grad[:, at].astype(F32) * gain[:, at].astype(F32)


def split_kernel(mine, got, *pieces):
    for index, piece in enumerate(pieces):
        piece[...] = mine[index] + got[index]


def join_kernel(skip, count, *refs):
    parts = refs[skip : skip + count]
    total = parts[0][...]
    for part in parts[1:]:
        total = total + part[...]
    refs[-1][...] = total


def members_kernel(reverse, group, rows, *refs):
    parts, refs = refs[:group], refs[group:]
    mirror, there, outs = refs[0], refs[1:rows], refs[rows:]
    row, low, high = here("row"), here("low"), here("high")
    ahead = jnp.where(before(1 - high, high, reverse), mirror[...], 0.0)
    for step in range(1, rows):
        sooner = before(row ^ step, row, reverse)
        ahead = ahead + jnp.where(sooner, there[step - 1][...], 0.0)
    for at, out in enumerate(outs):
        result = ahead
        for step in range(group):
            if step != at:
                sooner = before(low ^ step, low ^ at, reverse)
                result = result + jnp.where(sooner, parts[step][...], 0.0)
        out[...] = result


def merge_kernel(reverse, steps, *refs):
    back, refs = refs[: len(steps)], refs[len(steps) :]
    mine, got, (own, theirs) = refs[:2], refs[2:4], refs[4:]
    first = before(here("core"), 1 - here("core"), reverse)
    for index, step in enumerate(steps):
        which = int(step not in STEPS[0])
        at = STEPS[which].index(step)
        own[index] = back[index][...] + jnp.where(first, 0.0, got[which][at])
        theirs[index] = back[index][...] + jnp.where(first, mine[which][at], 0.0)


def forward_kernel(part, steps, last, queries, upstream, within, state, sooner, *refs):
    outputs = 3 if last else 4
    earlier, (output, low, *sums) = refs[:-outputs], refs[-outputs:]
    heads = sooner.shape[0]
    tokens = queries.shape[0]
    if earlier:
        square, mixed = (ref[...] for ref in earlier)
    else:
        square = mixed = jnp.zeros((tokens, HEAD_DIM), F32)
    for index, step in enumerate(steps):
        at = columns_of(part, step, heads)
        carried = []
        for block, rows in enumerate(blocks(tokens)):
            wide = state[index]
            if block:
                wide = wide + sooner[owner() ^ step, block - 1]
            state_low = wide.astype(BF16)
            low[index, block] = state_low
            carried.append(dot_nn(queries[rows, at], state_low))
        out = within[:, at] + FACTOR * jnp.concatenate(carried)
        output[:, columns(index)] = out
        square = square + out * out
        mixed = mixed + upstream[:, at] * out
    for row, array in enumerate((square, mixed)):
        if last:
            sums[0][row : row + 1] = jnp.sum(array.T, axis=0, keepdims=True)
        else:
            sums[row][...] = array


def delta_kernel(part, queries, upstream, output_a, output_b, *refs):
    sums, (delta, first, rest, later) = refs[:4], refs[4:]
    tokens = queries.shape[0]
    heads = delta.shape[1] // HEAD_DIM
    total = sums[0][...] + sums[1][...] + sums[2][...] + sums[3][...]
    inv_rms = lax.rsqrt(total[0:1] / FEATURES + EPSILON)
    pull = inv_rms * inv_rms * inv_rms * (total[1:2] / FEATURES)
    inv_rms = jnp.broadcast_to(inv_rms, (HEAD_DIM, tokens)).T
    pull = jnp.broadcast_to(pull, (HEAD_DIM, tokens)).T
    for back, steps in zip((first, rest), STEPS):
        for index, step in enumerate(steps):
            which = int(step not in BACK[0])
            output = (output_a, output_b)[which][:, columns(BACK[which].index(step))]
            at = columns_of(part, step, heads)
            out_delta = (inv_rms * upstream[:, at] - pull * output).astype(BF16)
            delta[:, columns_of(0, step, heads)] = out_delta
            total = jnp.zeros(back.shape[1:], F32)
            parts = blocks(tokens)
            for block in reversed(range(len(parts))):
                rows = parts[block]
                if block + 1 < len(parts):
                    later[owner() ^ step, block] = total
                total = total + dot_tn(out_delta[rows], queries[rows, at])
            back[index] = total


def write(near, far, part, sem):
    half = near.shape[1]
    core = 1 - here("core") if part else here("core")
    there = pl.ds(pl.multiple_of(core * half, half), half)
    copy = pltpu.make_async_copy(near, far.at[:, there], sem)
    copy.start()
    return copy


def query_kernel(*refs):
    *operands, _, far, near_0, near_1, sems = refs
    mask = causal(operands[0].shape[0], False)
    copies = []
    for part, near in enumerate((near_0, near_1)):
        keys, values, delta, *lows = operands[part::2]
        heads = near.shape[1] // HEAD_DIM
        for low, steps in zip(lows, BACK):
            for index, step in enumerate(steps):
                at = columns_of(0, step, heads)
                out_delta = delta[:, at]
                carried = [
                    dot_nt(out_delta[rows], low[index, block])
                    for block, rows in enumerate(blocks(keys.shape[0]))
                ]
                delta_scores = scores(out_delta, values[:, at], mask)
                grad = dot_nn(delta_scores, keys[:, at]) + FACTOR * jnp.concatenate(carried)
                near[:, at] = grad.astype(BF16)
        copies.append(write(near, far, part, sems.at[part]))
    for copy in copies:
        copy.wait()


def inner_kernel(part, queries, keys, values, delta, after, key_inner, value_inner):
    del after
    mask = causal(keys.shape[0], True)
    heads = delta.shape[1] // HEAD_DIM
    for head in range(heads):
        at = columns(head)
        query, out_delta = queries[:, columns(part * heads + head)], delta[:, at]
        key_inner[:, at] = dot_nn(scores(values[:, at], out_delta, mask), query)
        value_inner[:, at] = dot_nn(scores(keys[:, at], query, mask), out_delta)


def head_grads(step, operands, state, key_near, value_near, near_at):
    keys, values, key_inner, value_inner, later = operands
    parts = blocks(keys.shape[0])
    at = columns_of(0, step, later.shape[0])
    lows = []
    for block in range(len(parts)):
        wide = state
        if block + 1 < len(parts):
            wide = wide + later[owner() ^ step, block]
        lows.append(wide.astype(BF16))
    carried = [dot_nn(values[rows, at], lows[n]) for n, rows in enumerate(parts)]
    grad = key_inner[:, at] + FACTOR * jnp.concatenate(carried)
    key_near[:, near_at] = grad.astype(BF16)
    carried = [dot_nt(keys[rows, at], lows[n]) for n, rows in enumerate(parts)]
    grad = value_inner[:, at] + FACTOR * jnp.concatenate(carried)
    value_near[:, near_at] = grad.astype(BF16)


def own_kernel(*refs):
    operands, states, nears = refs[:5], refs[5:7], refs[7:]
    for state, steps in zip(states, BACK):
        for index, step in enumerate(steps):
            at = columns_of(0, step, operands[4].shape[0])
            head_grads(step, operands, state[index], *nears, at)


def backward_kernel(steps, *refs):
    operands, state, nears = refs[:5], refs[5], refs[6:]
    for index, step in enumerate(steps):
        head_grads(step, operands, state[index], *nears, columns(index))


def last_kernel(*refs):
    operands, (key_0, value_0, key_1, value_1), refs = refs[:6], refs[6:10], refs[10:]
    (key_far, value_far), (key_last, value_last, sems) = refs[:2], refs[2:]
    heads = operands[4].shape[0]
    copies = [
        write(key_0, key_far, 0, sems.at[0]),
        write(value_0, value_far, 0, sems.at[1]),
    ]

    def send(steps, pair):
        for near, far in zip(pair, (key_far, value_far)):
            for index, step in enumerate(steps):
                there = columns_of(1 - here("core"), step, heads)
                copy = pltpu.make_async_copy(
                    near.at[:, columns(index)], far.at[:, there], sems.at[len(copies)]
                )
                copy.start()
                copies.append(copy)

    send(BACK[0], (key_1, value_1))
    backward_kernel(BACK[1], *operands, key_last, value_last)
    send(BACK[1], (key_last, value_last))
    for copy in copies:
        copy.wait()


def swap(array, axis, distance):
    count = lax.axis_size(axis)
    return lax.ppermute(array, axis, [(at, at ^ distance) for at in range(count)])


def before(one, other, reverse):
    return one > other if reverse else one < other


def owner():
    return here("low") ^ (lax.axis_size("low") // 2 * here("high"))


def swaps(arrays, axis, order):
    there = {step: swap(arrays[step], axis, step) for step in order}
    return [there[step] for step in sorted(there)]


def entering(mine, other, reverse, beside):
    group, rows = lax.axis_size("low"), lax.axis_size("row")
    line, ring = (3, 2, 1), (1, 3, 2)
    piece = near(mine[0].shape[1:])
    got = [swap(array, "core", 1) for array in other]
    parts = {}
    for steps, *arrays in zip(STEPS, mine, got):
        parts.update(zip(steps, call(split_kernel, [piece] * len(steps))(*arrays)))
    made = beside(parts[0])
    parts = [parts[0]] + swaps(parts, "low", line)
    first, *ties = made
    whole = call(functools.partial(join_kernel, int(reverse), group), piece, far=int(reverse))(
        *((first, *parts) if reverse else (*parts, first)), *ties
    )
    mirror = swap(whole, ("high", "low"), group + group // 2)
    whole = call(functools.partial(join_kernel, 0, 2), piece)(whole, mirror)
    there = swaps([whole] * rows, "row", ring)
    back = call(functools.partial(members_kernel, reverse, group, rows), [piece] * group)(
        *parts, mirror, *there
    )
    back = [back[0]] + swaps(back, "low", line)
    states = []
    for steps in BACK:
        shape = near((len(steps), *mine[0].shape[1:]))
        own, theirs = call(functools.partial(merge_kernel, reverse, steps), (shape, shape))(
            *(back[step] for step in steps), *mine, *got
        )
        states.append((own, swap(theirs, "core", 1)))
    return list(zip(*states)), made


def on_device(queries, keys, values, out_grad, gain):
    tokens, width = queries.shape
    heads = width // HEAD_DIM
    gain = gain.reshape(1, width)
    wide = near((tokens, width), BF16)
    full = near((tokens, width))
    count = heads // 2
    states = [near((len(steps), HEAD_DIM, HEAD_DIM)) for steps in STEPS]
    inner_blocks = near((count, tokens // BLOCK - 1, HEAD_DIM, HEAD_DIM))
    half_wide = near((tokens, width // 2), BF16)
    half_full = near((tokens, width // 2))
    lane_full = near((tokens, HEAD_DIM))
    grads = pltpu.HBM((tokens, width), BF16)
    *other, sooner_1, keys_0, keys_1, values_0, values_1 = call(
        other_totals_kernel,
        (*states, inner_blocks, *[half_wide] * 4),
        far=2,
        scratch_shapes=[pltpu.SemaphoreType.DMA((2, 2, 1))],
    )(keys, values)
    *mine, sooner_0 = call(key_value_states, (*states, inner_blocks))(keys_0, values_0)
    sooner, keys, values = (sooner_0, sooner_1), (keys_0, keys_1), (values_0, values_1)

    def beside_forward(after):
        return call(
            within_kernel,
            (full, full, wide),
            far=3,
            scratch_shapes=[wide, near((1, width), BF16), pltpu.SemaphoreType.DMA((3, 2))],
        )(queries, out_grad, gain, *keys, *values, after)

    entered, (within, upstream, queries) = entering(mine, other, False, beside_forward)
    outputs, lows, sums = [], [], []
    for part in range(2):
        for turn, steps in enumerate(BACK):
            last = bool(part and turn)
            output, low, *sums = call(
                functools.partial(forward_kernel, part, steps, last),
                (
                    near((tokens, len(steps) * HEAD_DIM)),
                    near((len(steps), tokens // BLOCK, HEAD_DIM, HEAD_DIM), BF16),
                    *([near((2, tokens))] if last else [lane_full] * 2),
                ),
            )(queries, upstream, within, entered[part][turn], sooner[part], *sums)
            outputs.append(output)
            lows.append(low)
    sums = swaps(sums * lax.axis_size("head"), "head", (1, 3, 2)) + sums
    results = [
        call(
            functools.partial(delta_kernel, part), (half_wide, *states, inner_blocks)
        )(queries, upstream, *outputs[2 * part : 2 * part + 2], *sums)
        for part in (1, 0)
    ][::-1]
    deltas = [result[0] for result in results]
    later = [result[3] for result in results]

    def beside_backward(after):
        query_grad = call(
            query_kernel,
            grads,
            scratch_shapes=[half_wide, half_wide, pltpu.SemaphoreType.DMA((2,))],
        )(*keys, *values, *deltas, *lows[::2], *lows[1::2], after)
        inner = [
            call(functools.partial(inner_kernel, part), (half_full, half_full))(
                queries, keys[part], values[part], deltas[part], after
            )
            for part in range(2)
        ]
        return query_grad, *inner[0], *inner[1]

    entered, (query_grad, *inner) = entering(
        results[0][1:3], results[1][1:3], True, beside_backward
    )
    own, theirs = (
        (keys[part], values[part], *inner[2 * part : 2 * part + 2], later[part])
        for part in range(2)
    )
    ready = list(call(own_kernel, (half_wide, half_wide))(*own, *entered[0]))
    shapes = [near((tokens, len(steps) * HEAD_DIM), BF16) for steps in BACK]
    ready += call(functools.partial(backward_kernel, BACK[0]), (shapes[0], shapes[0]))(
        *theirs, entered[1][0]
    )
    key_grad, value_grad = call(
        last_kernel,
        (grads, grads),
        scratch_shapes=[shapes[1], shapes[1], pltpu.SemaphoreType.DMA((2 + heads,))],
    )(*theirs, entered[1][1], *ready)
    return query_grad, key_grad, value_grad


def solution(mesh):
    _, across = mesh.devices.shape
    shape = (4, 2, 4, 2, across)
    inner = Mesh(mesh.devices.reshape(shape), ("row", "high", "low", "core", "head"))
    spec = P(("row", "high", "low", "core"), "head")
    return jax.shard_map(
        on_device,
        mesh=inner,
        in_specs=(spec, spec, spec, spec, P("head")),
        out_specs=(spec, spec, spec),
        check_vma=False,
    )
```
